512 devices in a mesh: prompt: 4 (over x), sample: 32 (over z, y_lo, core), head: 4 (over y_hi).
Axes of the slice: x: 4, y: 8 (y_hi: 4, y_lo: 2; y = y_hi * 2 + y_lo), z: 8, core: 2. Of those that a mesh axis runs over, the one named last changes fastest.
Arguments:
- comp_q: bfloat16 [4, 32, 128, 4096], P('prompt', 'sample', None, 'head'), may hold values from -6 to 6
- comp_k: bfloat16 [4, 32, 128, 512], P('prompt', 'sample', None, 'head'), may hold values from -6 to 6
- comp_v: bfloat16 [4, 32, 128, 512], P('prompt', 'sample', None, 'head'), may hold values from -6 to 6
- prompt_k: bfloat16 [4, 3072, 512], P('prompt', 'sample', 'head'), may hold values from -6 to 6
- prompt_v: bfloat16 [4, 3072, 512], P('prompt', 'sample', 'head'), may hold values from -6 to 6
- lengths: int32 [4, 32], P('prompt', 'sample'), may hold values from 64 to 128, as said below
- q_gain: float32 [128], replicated, may hold values from 0.5 to 4
- k_gain: float32 [128], replicated, may hold values from 0.5 to 4
- d_out: bfloat16 [4, 32, 128, 4096], P('prompt', 'sample', None, 'head'), may hold values from -6 to 6
Outputs:
- attn_out: bfloat16 [4, 32, 128, 4096], P('prompt', 'sample', None, 'head')
- d_q: bfloat16 [4, 32, 128, 4096], P('prompt', 'sample', None, 'head')
- d_comp_k: bfloat16 [4, 32, 128, 512], P('prompt', 'sample', None, 'head')
- d_comp_v: bfloat16 [4, 32, 128, 512], P('prompt', 'sample', None, 'head')
- d_prompt_k: bfloat16 [4, 3072, 512], P('prompt', 'sample', 'head')
- d_prompt_v: bfloat16 [4, 3072, 512], P('prompt', 'sample', 'head')
- gain_grads: float32 [2, 128], replicated
The draws below stay inside these ranges and needn't reach their ends.
Inputs may be any that keep to these rules, and one draw needn't show every extreme that they name: `lengths`: multiples of 64; in every group one completion has 128 live tokens and another 64.
All inputs are finite; a program needn't handle non-finite values.
Results may differ from the reference program's by a relative error of at most 0.03.
Values may be sent and summed in bfloat16 or wider, within the bound.
A program may use at most 64 MiB of HBM per device.

```python
import math
import jax
import jax.numpy as jnp
from jax import lax

HQ = 32
HK = 4
DH = 128
LEN_STEP = 64
CLEN = 128
GROUPS = 4
COMPS = 32
PROMPT = 3072


def prompt_key_base(key):
    return jax.random.truncated_normal(jax.random.fold_in(key, 101), -6.0, 6.0, (GROUPS, PROMPT, HK * DH), jnp.float32)


def draw_prompt_k(key, part):
    shared = prompt_key_base(key)
    return shared.astype(jnp.bfloat16)


def draw_comp_q(key, part):
    key = jax.random.fold_in(key, 5)
    queries = jax.random.truncated_normal(key, -6.0, 6.0, (GROUPS, COMPS, CLEN, HQ * DH), jnp.float32)
    return queries.astype(jnp.bfloat16)


def gain_values(key, lower, upper):
    return jnp.exp(jax.random.uniform(key, (DH,), jnp.float32, math.log(lower), math.log(upper)))


def draw_q_gain(key, part):
    key = jax.random.fold_in(key, 7)
    return gain_values(key, 0.5, 2.0)


def draw_k_gain(key, part):
    key = jax.random.fold_in(key, 9)
    return gain_values(key, 0.5, 2.0)


def draw_lengths(key, part):
    key = jax.random.fold_in(key, 11)
    key_vals, key_full, key_short = jax.random.split(key, 3)
    steps_all = CLEN // LEN_STEP
    drawn = jax.random.randint(key_vals, (GROUPS, COMPS), 1, steps_all + 1) * LEN_STEP
    full_at = jax.random.randint(key_full, (GROUPS, 1), 0, COMPS)
    short_at = (full_at + jax.random.randint(key_short, (GROUPS, 1), 1, COMPS)) % COMPS
    comp_ids = jnp.arange(COMPS, dtype=jnp.int32)[None, :]
    drawn = jnp.where(comp_ids == full_at, CLEN, drawn)
    drawn = jnp.where(comp_ids == short_at, LEN_STEP, drawn)
    return drawn.astype(jnp.int32)


def levels(rng, dims, shards, smallest, largest):
    gain = 1.0
    for dim, parts in shards:
        draws = jax.random.uniform(jax.random.fold_in(jax.random.fold_in(rng, 6), dim), (parts,), jnp.float32, smallest / len(shards), largest / len(shards))
        gain = gain * jnp.repeat(jnp.exp(draws), dims[dim] // parts).reshape((-1,) + (1,) * (len(dims) - 1 - dim))
    return gain


def bell_draw(key, dims, deviation, most, pieces=(), held_as=jnp.bfloat16):
    values = deviation * jax.random.normal(key, dims, jnp.float32)
    if pieces:
        values = values * levels(key, dims, pieces, -0.22, 0.18)
    return jnp.clip(values, -most, most).astype(held_as)


def setup_inputs(seed: int = 0) -> dict:
    streams_of = jax.random.split(jax.random.key(seed), 10)
    return {
        "comp_q": draw_comp_q(jax.random.fold_in(streams_of[9], 71), 0),
        "comp_k": bell_draw(streams_of[1], (GROUPS, COMPS, CLEN, HK * DH), 1.0, 6.0, ((0, 4), (1, 32), (3, 4))),
        "comp_v": bell_draw(streams_of[2], (GROUPS, COMPS, CLEN, HK * DH), 1.0, 6.0, ((0, 4), (1, 32), (3, 4))),
        "prompt_k": draw_prompt_k(jax.random.fold_in(streams_of[9], 71), 0),
        "prompt_v": bell_draw(streams_of[4], (GROUPS, PROMPT, HK * DH), 1.0, 6.0, ((0, 4), (1, 32), (2, 4))),
        "lengths": draw_lengths(jax.random.fold_in(streams_of[9], 71), 0),
        "q_gain": draw_q_gain(jax.random.fold_in(streams_of[9], 71), 0),
        "k_gain": draw_k_gain(jax.random.fold_in(streams_of[9], 71), 0),
        "d_out": bell_draw(streams_of[8], (GROUPS, COMPS, CLEN, HQ * DH), 1.0, 6.0, ((0, 4), (1, 32), (3, 4))),
    }


EPS = 1e-06

def normalize(inputs, gain_vec):
    inverse_rms = lax.rsqrt(lax.optimization_barrier(jnp.mean(inputs * inputs, axis=-1, keepdims=True)) + EPS)
    return inputs * inverse_rms * gain_vec

def normalize_back(inputs, gain_vec, upstream):
    _, pullback = jax.vjp(normalize, inputs, gain_vec)
    return pullback(upstream)

def rounded(values):
    return lax.optimization_barrier(values.astype(jnp.bfloat16)).astype(jnp.float32)

def completion_terms(q_norm, prompt_norm, prompt_vals, comp_norm, comp_vals, live_count, grad_in, score_scale):
    comp_len = q_norm.shape[0]
    prompt = prompt_norm.shape[0]
    all_keys = jnp.concatenate([prompt_norm, comp_norm], 0).astype(jnp.float32)
    all_vals = jnp.concatenate([prompt_vals, comp_vals], 0).astype(jnp.float32)
    query_f = q_norm.astype(jnp.float32)
    logits = jnp.einsum('qkgd,jkd->kgqj', query_f, all_keys) * score_scale
    row_ids = jnp.arange(comp_len, dtype=jnp.int32)[:, None]
    col_ids = jnp.arange(prompt + comp_len, dtype=jnp.int32)[None, :]
    allowed = (col_ids < prompt) | (col_ids - prompt <= row_ids)
    logits = jnp.where(allowed, logits, -jnp.inf)
    row_max = lax.optimization_barrier(jnp.max(logits, axis=-1, keepdims=True))
    log_norm = row_max + jnp.log(lax.optimization_barrier(jnp.sum(jnp.exp(logits - row_max), axis=-1, keepdims=True)))
    attn_prob = jnp.exp(logits - log_norm)
    prob_round = rounded(attn_prob)
    mixture = jnp.einsum('kgqj,jkd->qkgd', prob_round, all_vals)
    live_rows = (jnp.arange(comp_len, dtype=jnp.int32) < live_count)[:, None, None, None]
    attended = jnp.where(live_rows, mixture, 0.0).astype(jnp.bfloat16)
    grad_out = jnp.where(live_rows, grad_in, jnp.zeros_like(grad_in))
    grad_f = grad_out.astype(jnp.float32)
    row_dot = lax.optimization_barrier(jnp.sum(grad_f * attended.astype(jnp.float32), axis=-1)).transpose(1, 2, 0)[..., None]
    dprob = jnp.einsum('qkgd,jkd->kgqj', grad_f, all_vals)
    dlogit = rounded(attn_prob * (dprob - row_dot))
    grad_query = jnp.einsum('kgqj,jkd->qkgd', dlogit, all_keys) * score_scale
    grad_key = jnp.einsum('kgqj,qkgd->jkd', dlogit, query_f) * score_scale
    grad_value = jnp.einsum('kgqj,qkgd->jkd', prob_round, grad_f)
    return (attended, grad_query, grad_key, grad_value)

def reference(comp_q, comp_k, comp_v, prompt_k, prompt_v, lengths, q_gain, k_gain, d_out):
    groups, comps, comp_len, q_width = comp_q.shape
    head_dim = q_gain.shape[0]
    q_heads = q_width // head_dim
    kv_heads = comp_k.shape[3] // head_dim
    group_size = q_heads // kv_heads
    prompt = prompt_k.shape[1]
    score_scale = 1.0 / math.sqrt(head_dim)

    def one_group(group_in):
        g_query, g_key, g_value, g_pkey, g_pvalue, g_lengths, g_grad = group_in
        prompt_raw = g_pkey.astype(jnp.float32).reshape(prompt, kv_heads, head_dim)
        prompt_norm = normalize(prompt_raw, k_gain).astype(jnp.bfloat16)
        prompt_vals = g_pvalue.reshape(prompt, kv_heads, head_dim)

        def one_comp(state_in, comp_in):
            acc_key, acc_value, gain_q, gain_k = state_in
            c_query, c_key, c_value, live_count, c_grad = comp_in
            query_raw = c_query.astype(jnp.float32).reshape(comp_len, kv_heads, group_size, head_dim)
            q_norm = normalize(query_raw, q_gain).astype(jnp.bfloat16)
            key_raw = c_key.astype(jnp.float32).reshape(comp_len, kv_heads, head_dim)
            comp_norm = normalize(key_raw, k_gain).astype(jnp.bfloat16)
            attended, grad_query, grad_key, grad_value = completion_terms(q_norm, prompt_norm, prompt_vals, comp_norm, c_value.reshape(comp_len, kv_heads, head_dim), live_count, c_grad.reshape(comp_len, kv_heads, group_size, head_dim), score_scale)
            dq_raw, gain_q_add = normalize_back(query_raw, q_gain, grad_query)
            dk_raw, gain_k_add = normalize_back(key_raw, k_gain, grad_key[prompt:])
            new_state = (acc_key + grad_key[:prompt], acc_value + grad_value[:prompt], gain_q + gain_q_add, gain_k + gain_k_add)
            per_comp = (attended.reshape(comp_len, q_width), dq_raw.astype(jnp.bfloat16).reshape(comp_len, q_width), dk_raw.astype(jnp.bfloat16).reshape(comp_len, kv_heads * head_dim), grad_value[prompt:].astype(jnp.bfloat16).reshape(comp_len, kv_heads * head_dim))
            return (new_state, per_comp)
        zeros_kv = jnp.zeros((prompt, kv_heads, head_dim), jnp.float32)
        zeros_gain = jnp.zeros((head_dim,), jnp.float32)
        final, per_comp = lax.scan(one_comp, (zeros_kv, zeros_kv, zeros_gain, zeros_gain), (g_query, g_key, g_value, g_lengths, g_grad))
        dpk_raw, gain_k_prompt = normalize_back(prompt_raw, k_gain, final[0])
        return per_comp + (dpk_raw.astype(jnp.bfloat16).reshape(prompt, kv_heads * head_dim), final[1].astype(jnp.bfloat16).reshape(prompt, kv_heads * head_dim), final[2], final[3] + gain_k_prompt)
    per_group = lax.map(one_group, (comp_q, comp_k, comp_v, prompt_k, prompt_v, lengths, d_out))
    row_count = groups * comps * comp_len * q_heads
    gain_grads = jnp.stack([lax.optimization_barrier(jnp.sum(per_group[6], axis=0)), lax.optimization_barrier(jnp.sum(per_group[7], axis=0))]) / math.sqrt(row_count)
    return (per_group[0], per_group[1], per_group[2], per_group[3], per_group[4], per_group[5], gain_grads)
```

```python
import functools
import math

import jax
import jax.numpy as jnp
from jax import lax
from jax.experimental import pallas as pl
from jax.experimental.pallas import tpu as pltpu
from jax.sharding import PartitionSpec as P

EPS = 1e-06
BF = jnp.bfloat16
F32 = jnp.float32
NT = (((1,), (1,)), ((), ()))
NN = (((1,), (0,)), ((), ()))
DH = 128
TOK = 128
QH = 8
NQ = TOK * QH
Q2 = 2 * NQ
OWN = 96
GR = 4 * OWN
NG = 4
KEYS = NG * GR
QB = 256
SCALE = 1.0 / math.sqrt(DH)
C2 = SCALE / math.log(2.0)
LOW = -1e30
MESH = pl.DeviceIdType.MESH


def dot(a, b, dims):
    return lax.dot_general(a, b, dims, preferred_element_type=F32)


def rms(x):
    return lax.rsqrt(jnp.mean(x * x, axis=-1, keepdims=True) + EPS)


def norm_back(x, gain, up):
    r = rms(x)
    g = up * gain
    return r * g - x * (r * r * r * jnp.mean(x * g, axis=-1, keepdims=True))


def row_near(d):
    return ((d - 1) * 4 + 2) * OWN


def row_far(d):
    return d * 4 * OWN


ROW_FAR0 = OWN
ROW_FAR4 = (3 * 4 + 3) * OWN


def kernel(
    cq, ck, cv, pk, pv, live_ref, q_gain, k_gain, d_out,
    out, dq, dck, dcv, dpk, dpv, gains,
    kv, q, do, ownkv, trans, s_buf, e_buf, dp_buf, e_own, dp_own, o_t, dq_t, o_rem, dq_rem, m_run,
    m_at, stat, stat_rem, fac, part, y_out, y_in, y4_out, y4_in, z_out, z_in, g_acc, g_buf,
    zp_s, zp_r, zm_s, zm_r, y_s, y_r, c_s, c_r, ry_s, ry_r, rp_s, rp_r, rm_s, rm_r, g_s, g_r,
):
    sample = lax.axis_index("sample")
    px = lax.axis_index("prompt")
    hy = lax.axis_index("head")
    core = lax.rem(sample, 2)
    y = lax.rem(sample // 2, 2)
    z = sample // 4

    def at(z_, y_, c_):
        return z_ * 4 + y_ * 2 + c_

    sib = {"sample": at(z, y, 1 - core)}
    ynb = {"sample": at(z, 1 - y, core)}
    zup = {"sample": at(lax.rem(z + 1, 8), y, core)}
    zdn = {"sample": at(lax.rem(z + 7, 8), y, core)}

    my_slot = (px * 2 + core, z, hy * 2 + y)

    def partner(r, i):
        if r == 0:
            return {"prompt": i // 2, "sample": at(z, y, lax.rem(i, 2))}
        if r == 1:
            return {"sample": at(i, y, core)}
        return {"head": i // 2, "sample": at(z, lax.rem(i, 2), core)}

    def send(src, dst, ss, rs, dev):
        return pltpu.make_async_remote_copy(
            src_ref=src, dst_ref=dst, send_sem=ss, recv_sem=rs, device_id=dev, device_id_type=MESH
        )

    barrier = pltpu.get_barrier_semaphore()
    for r in range(3):
        for k in range(1, 8):
            pl.semaphore_signal(
                barrier, inc=1, device_id=partner(r, lax.rem(my_slot[r] + k, 8)), device_id_type=MESH
            )

    kg = k_gain[...]
    qg = q_gain[...]
    pk_raw = pk[...].astype(F32)
    kv[0:OWN, 0:DH] = (pk_raw * rms(pk_raw) * kg).astype(BF)
    kv[0:OWN, DH:] = pv[...]
    pl.semaphore_wait(barrier, 21)

    def rows(start, count=OWN):
        return kv.at[pl.ds(start, count), :]

    def copy_zp(d, src):
        return send(rows(src), rows(row_near(d)), zp_s.at[d - 1], zp_r.at[d - 1], zdn)

    def copy_zm(d, src):
        return send(rows(src), rows(row_near(d) + OWN), zm_s.at[d - 1], zm_r.at[d - 1], zup)

    def copy_y(i, src, dst):
        return send(rows(src), rows(dst), y_s.at[i], y_r.at[i], ynb)

    copy_zp(1, 0).start()
    copy_zm(1, 0).start()
    copy_y(0, 0, ROW_FAR0).start()

    live = live_ref[0, 0]
    live_rows = lax.broadcasted_iota(jnp.int32, (TOK, 1), 0) < live
    for h in range(QH):
        x = cq[:, h * DH : (h + 1) * DH].astype(F32)
        q[h * TOK : (h + 1) * TOK, :] = (x * rms(x) * qg).astype(BF)
        g = d_out[:, h * DH : (h + 1) * DH]
        do[h * TOK : (h + 1) * TOK, :] = jnp.where(live_rows, g, jnp.zeros_like(g))
    copy_q = send(q.at[0:NQ, :], q.at[NQ:, :], c_s.at[0], c_r.at[0], sib)
    copy_do = send(do.at[0:NQ, :], do.at[NQ:, :], c_s.at[1], c_r.at[1], sib)
    copy_q.start()
    copy_do.start()

    ck_raw = ck[...].astype(F32)
    ownkv[:, 0:DH] = (ck_raw * rms(ck_raw) * kg).astype(BF)
    ownkv[:, DH:] = cv[...]

    m_run[...] = jnp.full((1, Q2), LOW, F32)
    stat[...] = jnp.zeros((8, Q2), F32)
    o_t[:, NQ:] = jnp.zeros((DH, NQ), F32)
    own_v_t = ownkv[:, DH:].astype(F32).T.astype(BF)
    trans[:, 0:TOK] = own_v_t
    u_ids = lax.broadcasted_iota(jnp.int32, (TOK, QB), 0)
    t_ids = lax.rem(lax.broadcasted_iota(jnp.int32, (TOK, QB), 1), TOK)
    allowed = u_ids <= t_ids
    for b in range(NQ // QB):
        sl = slice(b * QB, (b + 1) * QB)
        s = jnp.where(allowed, dot(ownkv[:, 0:DH], q[sl, :], NT), LOW)
        dp = dot(ownkv[:, DH:], do[sl, :], NT)
        m = jnp.max(s, axis=0, keepdims=True)
        e = jnp.exp2((s - m) * C2)
        eb = e.astype(BF)
        e_own[:, sl] = eb
        dp_own[:, sl] = dp
        m_run[:, sl] = m
        stat[1:2, sl] = jnp.sum(e, axis=0, keepdims=True)
        stat[2:3, sl] = jnp.sum(e * dp, axis=0, keepdims=True)
        o_t[:, sl] = dot(trans[:, 0:TOK], eb, NN)
    m_at[NG] = m_run[...]

    copy_q.wait_recv()
    copy_do.wait_recv()

    def forward(g, carry):
        near = row_near(g + 1)
        copy_zp(g + 1, near).wait_recv()

        @pl.when(g < 3)
        def _():
            copy_zp(g + 2, near).start()
            copy_y(g + 1, near, row_far(g + 1)).start()
            copy_zm(g + 1, near).wait_recv()
            copy_y(g + 4, near + OWN, row_far(g + 1) + OWN).start()

        @pl.when(g < 2)
        def _():
            copy_zm(g + 2, near + OWN).start()

        @pl.when(g == 3)
        def _():
            copy_y(7, near, ROW_FAR4).start()

        @pl.when(g == 0)
        def _():
            copy_y(0, 0, ROW_FAR0).wait_recv()

        @pl.when(g > 0)
        def _():
            copy_y(g, 0, row_far(g)).wait_recv()
            copy_y(g + 3, 0, row_far(g) + OWN).wait_recv()

        @pl.when(g == 3)
        def _():
            copy_y(7, 0, ROW_FAR4).wait_recv()

        at_rows = pl.ds(pl.multiple_of(g * GR, GR), GR)
        keys = kv[at_rows, 0:DH]
        vals = kv[at_rows, DH:]
        trans[...] = vals.astype(F32).T.astype(BF)
        tiles = Q2 // QB
        mx, al, mc, zs, ds = {}, {}, {}, {}, {}

        def sl(b):
            return slice(b * QB, (b + 1) * QB)

        for t in range(tiles + 2):
            if 1 <= t <= tiles:
                b = t - 1
                m_old = m_run[:, sl(b)]
                m_new = jnp.maximum(m_old, mx[b])
                m_run[:, sl(b)] = m_new
                al[b] = jnp.exp2((m_old - m_new) * C2)
                mc[b] = m_new * C2
            if t < tiles:
                s = dot(keys, q[sl(t), :], NT)
                s_buf[:, sl(t)] = s
                mx[t] = jnp.max(s, axis=0, keepdims=True)
                dp_buf[at_rows, sl(t)] = dot(vals, do[sl(t), :], NT)
            if 1 <= t <= tiles:
                b = t - 1
                e = jnp.exp2(s_buf[:, sl(b)] * C2 - mc[b])
                e_buf[at_rows, sl(b)] = e.astype(BF)
                stat[1:2, sl(b)] = stat[1:2, sl(b)] * al[b] + jnp.sum(e, axis=0, keepdims=True)
                stat[2:3, sl(b)] = stat[2:3, sl(b)] * al[b] + jnp.sum(
                    e * dp_buf[at_rows, sl(b)], axis=0, keepdims=True
                )
            if t >= 2:
                b = t - 2
                o_t[:, sl(b)] = o_t[:, sl(b)] * al[b] + dot(trans[...], e_buf[at_rows, sl(b)], NN)
        m_at[g] = m_run[...]
        return carry

    lax.fori_loop(0, NG, forward, 0)

    stat[0:1, :] = m_run[...]
    copy_st = send(stat, stat_rem, c_s.at[2], c_r.at[2], sib)
    copy_st.start()
    dq_t[...] = jnp.zeros((DH, Q2), F32)
    g_acc[...] = jnp.zeros((8, DH), F32)
    z_in[3, OWN:, :] = jnp.zeros((OWN, 2 * DH), BF)
    copy_st.wait_recv()
    for half in range(2):
        mine = slice(half * NQ, (half + 1) * NQ)
        other = slice((1 - half) * NQ, (2 - half) * NQ)
        m_a, m_b = stat[0:1, mine], stat_rem[0:1, other]
        m_f = jnp.maximum(m_a, m_b)
        w_a, w_b = jnp.exp2((m_a - m_f) * C2), jnp.exp2((m_b - m_f) * C2)
        inv = 1.0 / (stat[1:2, mine] * w_a + stat_rem[1:2, other] * w_b)
        for i in range(NG + (1 - half)):
            fac[i, :, mine] = jnp.exp2((m_at[i, :, mine] - m_f) * C2) * inv
        fac[NG + 1, :, mine] = (stat[2:3, mine] * w_a + stat_rem[2:3, other] * w_b) * inv
        o_t[:, mine] = o_t[:, mine] * (w_a * inv)
    copy_o = send(o_t.at[:, NQ:], o_rem, c_s.at[3], c_r.at[3], sib)
    copy_o.start()

    def copy_ry(g):
        return send(y_out.at[g], y_in.at[g], ry_s.at[g], ry_r.at[g], ynb)

    copy_ry0 = send(y_out.at[0, OWN:, :], y_in.at[0, OWN:, :], ry_s.at[0], ry_r.at[0], ynb)
    copy_ry4 = send(y4_out, y4_in, ry_s.at[4], ry_r.at[4], ynb)

    def copy_rp(g):
        return send(z_out.at[g, 0:OWN, :], z_in.at[g, 0:OWN, :], rp_s.at[g], rp_r.at[g], zup)

    def copy_rm(g):
        return send(z_out.at[g, OWN:, :], z_in.at[g, OWN:, :], rm_s.at[g], rm_r.at[g], zdn)

    def backward(i, carry):
        g = NG - 1 - i
        at_rows = pl.ds(pl.multiple_of(g * GR, GR), GR)
        keys = kv[at_rows, 0:DH]
        trans[...] = keys.astype(F32).T.astype(BF)
        dk = jnp.zeros((GR, DH), F32)
        dv = jnp.zeros((GR, DH), F32)
        for b in range(Q2 // QB):
            sl = slice(b * QB, (b + 1) * QB)
            p = e_buf[at_rows, sl].astype(F32) * fac[g, :, sl]
            pb = p.astype(BF)
            ds = (p * (dp_buf[at_rows, sl] - fac[NG + 1, :, sl])).astype(BF)
            dv = dv + dot(pb, do[sl, :], NN)
            dk = dk + dot(ds, q[sl, :], NN)
            dq_t[:, sl] += dot(trans[...], ds, NN)
        part[:, 0:DH] = dk
        part[:, DH:] = dv
        g_acc[...] += jnp.sum((dk * keys.astype(F32)).reshape(GR // 8, 8, DH), axis=0)

        y_out[g] = part[0 : 2 * OWN, :].astype(BF)

        @pl.when(g > 0)
        def _():
            copy_ry(g).start()

        @pl.when(g == 0)
        def _():
            copy_ry0.start()

        @pl.when(g == 3)
        def _():
            y4_out[...] = part[3 * OWN :, :].astype(BF)
            copy_ry4.start()
            copy_ry4.wait_recv()
            z_out[3, 0:OWN, :] = (part[2 * OWN : 3 * OWN, :] + y4_in[...].astype(F32)).astype(BF)
            copy_rp(3).start()

        @pl.when(g < 3)
        def _():
            copy_ry(g + 1).wait_recv()
            copy_rp(g + 1).wait_recv()

            @pl.when(g < 2)
            def _():
                copy_rm(g + 1).wait_recv()

            z_out[g] = (
                part[2 * OWN :, :] + y_in[g + 1].astype(F32) + z_in[g + 1].astype(F32)
            ).astype(BF)
            copy_rp(g).start()
            copy_rm(g).start()

        return carry

    lax.fori_loop(0, NG, backward, 0)

    copy_dq = send(dq_t.at[:, NQ:], dq_rem, c_s.at[4], c_r.at[4], sib)
    copy_dq.start()

    trans[:, 0:TOK] = ownkv[:, 0:DH].astype(F32).T.astype(BF)
    dk = jnp.zeros((TOK, DH), F32)
    dv = jnp.zeros((TOK, DH), F32)
    for b in range(NQ // QB):
        sl = slice(b * QB, (b + 1) * QB)
        p = e_own[:, sl].astype(F32) * fac[NG, :, sl]
        pb = p.astype(BF)
        ds = (p * (dp_own[:, sl] - fac[NG + 1, :, sl])).astype(BF)
        dv = dv + dot(pb, do[sl, :], NN)
        dk = dk + dot(ds, q[sl, :], NN)
        dq_t[:, sl] += dot(trans[:, 0:TOK], ds, NN)
    g_part = g_acc[...] + jnp.sum(
        (dk * ownkv[:, 0:DH].astype(F32)).reshape(TOK // 8, 8, DH), axis=0
    )

    def g_copy(r, i, dev):
        return send(g_buf.at[r, i], g_buf.at[r, i], g_s.at[r, i], g_r.at[r, i], dev)

    def g_start(r, value):
        g_buf[r, my_slot[r]] = value
        for k in range(1, 8):
            j = lax.rem(my_slot[r] + k, 8)
            pltpu.make_async_remote_copy(
                src_ref=g_buf.at[r, my_slot[r]],
                dst_ref=g_buf.at[r, my_slot[r]],
                send_sem=g_s.at[r, k],
                recv_sem=g_r.at[r, my_slot[r]],
                device_id=partner(r, j),
                device_id_type=MESH,
            ).start()

    def g_wait(r):
        for k in range(1, 8):
            j = lax.rem(my_slot[r] + k, 8)
            send(
                g_buf.at[r, j], g_buf.at[r, j], g_s.at[r, k], g_r.at[r, j], partner(r, j)
            ).wait_recv()
        total = g_buf[r, 0]
        for k in range(1, 8):
            total = total + g_buf[r, k]
        return total

    g_start(0, g_part)
    dck[...] = norm_back(ck_raw, kg, dk * SCALE).astype(BF)
    dcv[...] = dv.astype(BF)

    copy_o.wait_recv()
    for h in range(QH // 2):
        sl = slice(h * TOK, (h + 1) * TOK)
        x = (o_t[:, sl] + o_rem[:, sl]).T
        out[:, h * DH : (h + 1) * DH] = jnp.where(live_rows, x, 0.0).astype(BF)
    g_start(1, g_wait(0))
    for h in range(QH // 2, QH):
        sl = slice(h * TOK, (h + 1) * TOK)
        x = (o_t[:, sl] + o_rem[:, sl]).T
        out[:, h * DH : (h + 1) * DH] = jnp.where(live_rows, x, 0.0).astype(BF)

    copy_ry0.wait_recv()
    copy_rp(0).wait_recv()
    copy_rm(0).wait_recv()
    z0 = z_in[0].astype(F32)
    total = part[0:OWN, :] + y_in[0, OWN:, :].astype(F32) + z0[0:OWN] + z0[OWN:]
    dpk[...] = norm_back(pk_raw, kg, total[:, 0:DH] * SCALE).astype(BF)
    dpv[...] = total[:, DH:].astype(BF)
    g_start(2, g_wait(1))

    copy_dq.wait_recv()
    for h in range(QH):
        sl = slice(h * TOK, (h + 1) * TOK)
        up = (dq_t[:, sl] + dq_rem[:, sl]).T * SCALE
        x = cq[:, h * DH : (h + 1) * DH].astype(F32)
        dq[:, h * DH : (h + 1) * DH] = norm_back(x, qg, up).astype(BF)

    g_sum = jnp.sum(g_wait(2), axis=0, keepdims=True) * (SCALE / math.sqrt(GAIN_ROWS))
    gains[0:1, :] = g_sum / qg
    gains[1:2, :] = g_sum / kg

    for d in range(1, 5):
        copy_zp(d, 0).wait_send()
    for d in range(1, 4):
        copy_zm(d, 0).wait_send()
    for i in range(8):
        copy_y(i, 0, 0).wait_send()
    copy_q.wait_send()
    copy_do.wait_send()
    copy_st.wait_send()
    copy_o.wait_send()
    copy_dq.wait_send()
    copy_ry0.wait_send()
    copy_ry4.wait_send()
    for g in range(1, NG):
        copy_ry(g).wait_send()
    for g in range(NG):
        copy_rp(g).wait_send()
    for g in range(NG - 1):
        copy_rm(g).wait_send()
    for r in range(3):
        for k in range(1, 8):
            j = lax.rem(my_slot[r] + k, 8)
            send(
                g_buf.at[r, my_slot[r]], g_buf.at[r, my_slot[r]], g_s.at[r, k], g_r.at[r, j], partner(r, j)
            ).wait_send()


GAIN_ROWS = 524288


def per_device(comp_q, comp_k, comp_v, prompt_k, prompt_v, lengths, q_gain, k_gain, d_out):
    vmem = pl.BlockSpec(memory_space=pltpu.VMEM)
    smem = pl.BlockSpec(memory_space=pltpu.SMEM)
    dma = pltpu.SemaphoreType.DMA
    width = QH * DH
    shapes = [
        jax.ShapeDtypeStruct((TOK, width), BF),
        jax.ShapeDtypeStruct((TOK, width), BF),
        jax.ShapeDtypeStruct((TOK, DH), BF),
        jax.ShapeDtypeStruct((TOK, DH), BF),
        jax.ShapeDtypeStruct((OWN, DH), BF),
        jax.ShapeDtypeStruct((OWN, DH), BF),
        jax.ShapeDtypeStruct((2, DH), F32),
    ]
    scratch = [
        pltpu.VMEM((KEYS, 2 * DH), BF),
        pltpu.VMEM((Q2, DH), BF),
        pltpu.VMEM((Q2, DH), BF),
        pltpu.VMEM((TOK, 2 * DH), BF),
        pltpu.VMEM((DH, GR), BF),
        pltpu.VMEM((GR, Q2), F32),
        pltpu.VMEM((KEYS, Q2), BF),
        pltpu.VMEM((KEYS, Q2), F32),
        pltpu.VMEM((TOK, NQ), BF),
        pltpu.VMEM((TOK, NQ), F32),
        pltpu.VMEM((DH, Q2), F32),
        pltpu.VMEM((DH, Q2), F32),
        pltpu.VMEM((DH, NQ), F32),
        pltpu.VMEM((DH, NQ), F32),
        pltpu.VMEM((1, Q2), F32),
        pltpu.VMEM((NG + 1, 1, Q2), F32),
        pltpu.VMEM((8, Q2), F32),
        pltpu.VMEM((8, Q2), F32),
        pltpu.VMEM((NG + 2, 1, Q2), F32),
        pltpu.VMEM((GR, 2 * DH), F32),
        pltpu.VMEM((NG, 2 * OWN, 2 * DH), BF),
        pltpu.VMEM((NG, 2 * OWN, 2 * DH), BF),
        pltpu.VMEM((OWN, 2 * DH), BF),
        pltpu.VMEM((OWN, 2 * DH), BF),
        pltpu.VMEM((NG, 2 * OWN, 2 * DH), BF),
        pltpu.VMEM((NG, 2 * OWN, 2 * DH), BF),
        pltpu.VMEM((8, DH), F32),
        pltpu.VMEM((3, 8, 8, DH), F32),
        dma((4,)), dma((4,)), dma((3,)), dma((3,)), dma((8,)), dma((8,)), dma((5,)), dma((5,)),
        dma((5,)), dma((5,)), dma((4,)), dma((4,)), dma((4,)), dma((4,)), dma((3, 8)), dma((3, 8)),
    ]
    res = pl.pallas_call(
        kernel,
        out_shape=shapes,
        in_specs=[vmem] * 5 + [smem] + [vmem] * 3,
        out_specs=[vmem] * 7,
        scratch_shapes=scratch,
        compiler_params=pltpu.CompilerParams(
            collective_id=0, has_side_effects=True, vmem_limit_bytes=56 * 2**20
        ),
    )(
        comp_q.reshape(TOK, width),
        comp_k.reshape(TOK, DH),
        comp_v.reshape(TOK, DH),
        prompt_k.reshape(OWN, DH),
        prompt_v.reshape(OWN, DH),
        lengths,
        q_gain.reshape(1, DH),
        k_gain.reshape(1, DH),
        d_out.reshape(TOK, width),
    )
    return (
        res[0].reshape(1, 1, TOK, width),
        res[1].reshape(1, 1, TOK, width),
        res[2].reshape(1, 1, TOK, DH),
        res[3].reshape(1, 1, TOK, DH),
        res[4].reshape(1, OWN, DH),
        res[5].reshape(1, OWN, DH),
        res[6],
    )


def solution(mesh):
    return jax.shard_map(
        per_device,
        mesh=mesh,
        in_specs=(
            P("prompt", "sample", None, "head"),
            P("prompt", "sample", None, "head"),
            P("prompt", "sample", None, "head"),
            P("prompt", "sample", "head"),
            P("prompt", "sample", "head"),
            P("prompt", "sample"),
            P(),
            P(),
            P("prompt", "sample", None, "head"),
        ),
        out_specs=(
            P("prompt", "sample", None, "head"),
            P("prompt", "sample", None, "head"),
            P("prompt", "sample", None, "head"),
            P("prompt", "sample", None, "head"),
            P("prompt", "sample", "head"),
            P("prompt", "sample", "head"),
            P(),
        ),
        check_vma=False,
    )
```

```python
import functools
import math

import jax
import jax.numpy as jnp
from jax import lax
from jax.experimental import pallas as pl
from jax.experimental.pallas import tpu as pltpu
from jax.sharding import PartitionSpec as P

EPS = 1e-06
BF = jnp.bfloat16
F32 = jnp.float32
NT = (((1,), (1,)), ((), ()))
NN = (((1,), (0,)), ((), ()))
DH = 128
TOK = 128
QH = 8
NQ = TOK * QH
Q2 = 2 * NQ
OWN = 96
GR = 4 * OWN
NG = 4
KEYS = NG * GR
QB = 256
SCALE = 1.0 / math.sqrt(DH)
C2 = SCALE / math.log(2.0)
LOW = -1e30
MESH = pl.DeviceIdType.MESH


def dot(a, b, dims):
    return lax.dot_general(a, b, dims, preferred_element_type=F32)


def rms(x):
    return lax.rsqrt(jnp.mean(x * x, axis=-1, keepdims=True) + EPS)


def norm_back(x, gain, up):
    r = rms(x)
    g = up * gain
    return r * g - x * (r * r * r * jnp.mean(x * g, axis=-1, keepdims=True))


def row_near(d):
    return ((d - 1) * 4 + 2) * OWN


def row_far(d):
    return d * 4 * OWN


ROW_FAR0 = OWN
ROW_FAR4 = (3 * 4 + 3) * OWN
HALF = OWN // 2


def kernel(
    cq_hbm, ck, cv, pk, pv, live_ref, q_gain, k_gain, dout_hbm,
    out_hbm, dq_hbm, dck_hbm, dcv_hbm, dpk_hbm, dpv_hbm, gains_hbm,
    cq, d_out, out, dq, dck, dcv, dpk, dpv, gains,
    kv, q, do, ownkv, trans, s_buf, e_buf, f_buf, dp_buf, e_own, dp_own, ok_t, dq_t, o_rem, dq_rem, m_run,
    m_at, stat, stat_rem, fac, part, y_out, y_in, y4_out, y4_in, z_out, z_in, g_buf,
    io_s, za_s, za_r, y_s, y_r, c_s, c_r, ry_s, ry_r, rz_s, rz_r, g_s, g_r,
):
    read_q = pltpu.make_async_copy(cq_hbm, cq, io_s.at[0])
    read_d = pltpu.make_async_copy(dout_hbm, d_out, io_s.at[1])
    read_q.start()
    read_d.start()

    sample = lax.axis_index("sample")
    px = lax.axis_index("prompt")
    hy = lax.axis_index("head")
    core = lax.rem(sample, 2)
    y = lax.rem(sample // 2, 2)
    z = sample // 4

    def at(z_, y_, c_):
        return z_ * 4 + y_ * 2 + c_

    sib = {"sample": at(z, y, 1 - core)}
    ynb = {"sample": at(z, 1 - y, core)}

    def z_dev(d):
        return {"sample": at(lax.rem(z + d + 8, 8), y, core)}

    my_slot = (px * 2 + core, z, hy * 2 + y)

    def partner(r, i):
        if r == 0:
            return {"prompt": i // 2, "sample": at(z, y, lax.rem(i, 2))}
        if r == 1:
            return {"sample": at(i, y, core)}
        return {"head": i // 2, "sample": at(z, lax.rem(i, 2), core)}

    def send(src, dst, ss, rs, dev):
        return pltpu.make_async_remote_copy(
            src_ref=src, dst_ref=dst, send_sem=ss, recv_sem=rs, device_id=dev, device_id_type=MESH
        )

    barrier = pltpu.get_barrier_semaphore()
    for r in (1, 2, 0):
        for k in range(1, 8):
            pl.semaphore_signal(
                barrier, inc=1, device_id=partner(r, lax.rem(my_slot[r] + k, 8)), device_id_type=MESH
            )

    kg = k_gain[...]
    qg = q_gain[...]
    pk_raw = pk[...].astype(F32)
    kv[0:OWN, 0:DH] = (pk_raw * rms(pk_raw) * kg).astype(BF)
    kv[0:OWN, DH:] = pv[...]
    pl.semaphore_wait(barrier, 21)

    def rows(start, count=OWN):
        return kv.at[pl.ds(start, count), :]

    z_plan = (
        (-1, row_near(1), 0, OWN),
        (1, row_near(1) + OWN, 0, OWN),
        (-2, row_near(2), 0, OWN),
        (2, row_near(2) + OWN, 0, OWN),
        (-1, row_near(3), row_near(2), OWN),
        (1, row_near(3) + OWN, row_near(2) + OWN, OWN),
        (-2, row_near(4), row_near(2), HALF),
        (2, row_near(4) + HALF, row_near(2) + OWN + HALF, HALF),
    )

    def copy_z(i):
        to, dst, src, count = z_plan[i]
        return send(rows(src, count), rows(dst, count), za_s.at[i], za_r.at[i], z_dev(to))

    y_plan = (
        [(ROW_FAR0, 0)]
        + [(row_far(d), row_near(d)) for d in (1, 2, 3)]
        + [(row_far(d) + OWN, row_near(d) + OWN) for d in (1, 2, 3)]
        + [(ROW_FAR4, row_near(4))]
    )

    def copy_y(i):
        dst, src = y_plan[i]
        return send(rows(src), rows(dst), y_s.at[i], y_r.at[i], ynb)

    for i in (2, 3, 0, 1):
        copy_z(i).start()
    copy_y(0).start()

    live = live_ref[0, 0]
    live_rows = lax.broadcasted_iota(jnp.int32, (TOK, 1), 0) < live
    read_q.wait()
    for h in range(QH):
        x = cq[:, h * DH : (h + 1) * DH].astype(F32)
        q[h * TOK : (h + 1) * TOK, :] = (x * rms(x) * qg).astype(BF)
    copy_q = send(q.at[0:NQ, :], q.at[NQ:, :], c_s.at[0], c_r.at[0], sib)
    copy_q.start()
    read_d.wait()
    for h in range(QH):
        g = d_out[:, h * DH : (h + 1) * DH]
        do[h * TOK : (h + 1) * TOK, :] = jnp.where(live_rows, g, jnp.zeros_like(g))
    copy_do = send(do.at[0:NQ, :], do.at[NQ:, :], c_s.at[1], c_r.at[1], sib)
    copy_do.start()

    ck_raw = ck[...].astype(F32)
    ownkv[:, 0:DH] = (ck_raw * rms(ck_raw) * kg).astype(BF)
    ownkv[:, DH:] = cv[...]

    def turn(keys, vals, count):
        trans[0:DH, 0:count] = vals.astype(F32).T.astype(BF)
        trans[DH:, 0:count] = keys.astype(F32).T.astype(BF)

    m_run[...] = jnp.full((1, Q2), LOW, F32)
    stat[...] = jnp.zeros((8, Q2), F32)
    ok_t[:, NQ:] = jnp.zeros((2 * DH, NQ), F32)
    dq_t[:, NQ:] = jnp.zeros((DH, NQ), F32)
    turn(ownkv[:, 0:DH], ownkv[:, DH:], TOK)
    u_ids = lax.broadcasted_iota(jnp.int32, (TOK, QB), 0)
    t_ids = lax.rem(lax.broadcasted_iota(jnp.int32, (TOK, QB), 1), TOK)
    allowed = u_ids <= t_ids
    for b in range(NQ // QB):
        sl = slice(b * QB, (b + 1) * QB)
        s = jnp.where(allowed, dot(ownkv[:, 0:DH], q[sl, :], NT), LOW)
        dp = dot(ownkv[:, DH:], do[sl, :], NT)
        m = jnp.max(s, axis=0, keepdims=True)
        e = jnp.exp2((s - m) * C2)
        eb = e.astype(BF)
        ed = e * dp
        e_own[:, sl] = eb
        dp_own[:, sl] = dp
        m_run[:, sl] = m
        stat[1:2, sl] = jnp.sum(e, axis=0, keepdims=True)
        stat[2:3, sl] = jnp.sum(ed, axis=0, keepdims=True)
        ok_t[:, sl] = dot(trans[:, 0:TOK], eb, NN)
        dq_t[:, sl] = dot(trans[DH:, 0:TOK], ed.astype(BF), NN)
    m_at[NG] = m_run[...]

    for i in range(4):
        copy_z(i).wait_recv()
    for i in range(4, 8):
        copy_z(i).start()
    for i in (1, 4, 2, 5):
        copy_y(i).start()
    copy_q.wait_recv()
    copy_do.wait_recv()

    def forward(g, carry):
        @pl.when(g == 0)
        def _():
            copy_y(0).wait_recv()

        @pl.when(g == 1)
        def _():
            copy_y(1).wait_recv()
            copy_y(4).wait_recv()

        @pl.when(g == 2)
        def _():
            copy_z(4).wait_recv()
            copy_z(5).wait_recv()
            copy_y(3).start()
            copy_y(6).start()
            copy_z(6).wait_recv()
            copy_z(7).wait_recv()
            copy_y(7).start()
            copy_y(2).wait_recv()
            copy_y(5).wait_recv()

        @pl.when(g == 3)
        def _():
            copy_y(3).wait_recv()
            copy_y(6).wait_recv()
            copy_y(7).wait_recv()

        at_rows = pl.ds(pl.multiple_of(g * GR, GR), GR)
        keys = kv[at_rows, 0:DH]
        vals = kv[at_rows, DH:]
        turn(keys, vals, GR)
        tiles = Q2 // QB
        mx, al, mc = {}, {}, {}

        def sl(b):
            return slice(b * QB, (b + 1) * QB)

        for t in range(tiles + 2):
            if 1 <= t <= tiles:
                b = t - 1
                m_old = m_run[:, sl(b)]
                m_new = jnp.maximum(m_old, mx[b])
                m_run[:, sl(b)] = m_new
                al[b] = jnp.exp2((m_old - m_new) * C2)
                mc[b] = m_new * C2
            if t < tiles:
                s = dot(keys, q[sl(t), :], NT)
                s_buf[:, sl(t)] = s
                mx[t] = jnp.max(s, axis=0, keepdims=True)
                dp_buf[at_rows, sl(t)] = dot(vals, do[sl(t), :], NT)
            if 1 <= t <= tiles:
                b = t - 1
                e = jnp.exp2(s_buf[:, sl(b)] * C2 - mc[b])
                ed = e * dp_buf[at_rows, sl(b)]
                e_buf[at_rows, sl(b)] = e.astype(BF)
                f_buf[:, sl(b)] = ed.astype(BF)
                stat[1:2, sl(b)] = stat[1:2, sl(b)] * al[b] + jnp.sum(e, axis=0, keepdims=True)
                stat[2:3, sl(b)] = stat[2:3, sl(b)] * al[b] + jnp.sum(ed, axis=0, keepdims=True)
            if t >= 2:
                b = t - 2
                ok_t[:, sl(b)] = ok_t[:, sl(b)] * al[b] + dot(trans[...], e_buf[at_rows, sl(b)], NN)
                dq_t[:, sl(b)] = dq_t[:, sl(b)] * al[b] + dot(trans[DH:, :], f_buf[:, sl(b)], NN)
        m_at[g] = m_run[...]
        return carry

    lax.fori_loop(0, NG, forward, 0)

    stat[0:1, :] = m_run[...]
    copy_st = send(stat, stat_rem, c_s.at[2], c_r.at[2], sib)
    copy_st.start()
    copy_st.wait_recv()
    for half in range(2):
        mine = slice(half * NQ, (half + 1) * NQ)
        other = slice((1 - half) * NQ, (2 - half) * NQ)
        m_a, m_b = stat[0:1, mine], stat_rem[0:1, other]
        m_f = jnp.maximum(m_a, m_b)
        w_a, w_b = jnp.exp2((m_a - m_f) * C2), jnp.exp2((m_b - m_f) * C2)
        inv = 1.0 / (stat[1:2, mine] * w_a + stat_rem[1:2, other] * w_b)
        for i in range(NG + (1 - half)):
            fac[i, :, mine] = jnp.exp2((m_at[i, :, mine] - m_f) * C2) * inv
        row_dot = (stat[2:3, mine] * w_a + stat_rem[2:3, other] * w_b) * inv
        fac[NG + 1, :, mine] = row_dot
        own = w_a * inv
        ok_t[0:DH, mine] = ok_t[0:DH, mine] * own
        dq_t[:, mine] = (dq_t[:, mine] - ok_t[DH:, mine] * row_dot) * own
    copy_dq = send(dq_t.at[:, NQ:], dq_rem, c_s.at[4], c_r.at[4], sib)
    copy_dq.start()
    copy_o = send(ok_t.at[0:DH, NQ:], o_rem, c_s.at[3], c_r.at[3], sib)
    copy_o.start()

    def g_start(r, value):
        g_buf[r, my_slot[r]] = value
        for k in range(1, 8):
            send(
                g_buf.at[r, my_slot[r]], g_buf.at[r, my_slot[r]], g_s.at[r, k], g_r.at[r, my_slot[r]],
                partner(r, lax.rem(my_slot[r] + k, 8)),
            ).start()

    def g_wait(r):
        for k in range(1, 8):
            j = lax.rem(my_slot[r] + k, 8)
            send(
                g_buf.at[r, j], g_buf.at[r, j], g_s.at[r, k], g_r.at[r, j], partner(r, j)
            ).wait_recv()
        total = g_buf[r, 0]
        for k in range(1, 8):
            total = total + g_buf[r, k]
        return total

    pairs = dot(dq_t[...].astype(BF), q[...], NN)
    eye = lax.broadcasted_iota(jnp.int32, (DH, DH), 0) == lax.broadcasted_iota(jnp.int32, (DH, DH), 1)
    g_start(0, jnp.sum(jnp.where(eye, pairs, 0.0).reshape(DH // 8, 8, DH), axis=0))

    def copy_ry(g):
        return send(y_out.at[g], y_in.at[g], ry_s.at[g], ry_r.at[g], ynb)

    copy_ry0 = send(y_out.at[0, OWN:, :], y_in.at[0, OWN:, :], ry_s.at[0], ry_r.at[0], ynb)
    copy_ry4 = send(y4_out, y4_in, ry_s.at[4], ry_r.at[4], ynb)

    rz_plan = (
        (1, 0, 0, OWN), (-1, 1, 0, OWN), (2, 2, 0, OWN), (-2, 3, 0, OWN),
        (1, 4, 0, OWN), (-1, 5, 0, OWN), (2, 6, 0, HALF), (-2, 6, HALF, HALF),
    )

    def copy_rz(i):
        to, slot, start, count = rz_plan[i]
        at_slot = (slot, pl.ds(start, count))
        return send(z_out.at[at_slot], z_in.at[at_slot], rz_s.at[i], rz_r.at[i], z_dev(to))

    def backward(i, carry):
        g = NG - 1 - i
        at_rows = pl.ds(pl.multiple_of(g * GR, GR), GR)
        dk = jnp.zeros((GR, DH), F32)
        dv = jnp.zeros((GR, DH), F32)
        for b in range(Q2 // QB):
            sl = slice(b * QB, (b + 1) * QB)
            p = e_buf[at_rows, sl].astype(F32) * fac[g, :, sl]
            pb = p.astype(BF)
            ds = (p * (dp_buf[at_rows, sl] - fac[NG + 1, :, sl])).astype(BF)
            dv = dv + dot(pb, do[sl, :], NN)
            dk = dk + dot(ds, q[sl, :], NN)
        part[g, :, 0:DH] = dk
        part[g, :, DH:] = dv
        y_out[g] = part[g, 0 : 2 * OWN, :].astype(BF)

        @pl.when(g > 0)
        def _():
            copy_ry(g).start()

        @pl.when(g == 0)
        def _():
            copy_ry0.start()

        @pl.when(g == 3)
        def _():
            y4_out[...] = part[3, 3 * OWN :, :].astype(BF)
            copy_ry4.start()

        @pl.when(g == 1)
        def _():
            copy_ry(3).wait_recv()
            acc = part[2, 2 * OWN :, :] + y_in[3].astype(F32)
            z_out[4] = acc[0:OWN].astype(BF)
            z_out[5] = acc[OWN:].astype(BF)
            copy_rz(4).start()
            copy_rz(5).start()
            copy_ry4.wait_recv()
            z_out[6] = (part[3, 2 * OWN : 3 * OWN, :] + y4_in[...].astype(F32)).astype(BF)
            copy_rz(6).start()
            copy_rz(7).start()

        return carry

    lax.fori_loop(0, NG, backward, 0)

    g_start(1, g_wait(0))
    copy_ry(1).wait_recv()
    acc1 = part[0, 2 * OWN :, :] + y_in[1].astype(F32)
    z_out[0] = acc1[0:OWN].astype(BF)
    z_out[1] = acc1[OWN:].astype(BF)
    copy_rz(0).start()
    copy_rz(1).start()

    dk = jnp.zeros((TOK, DH), F32)
    dv = jnp.zeros((TOK, DH), F32)
    for b in range(NQ // QB):
        sl = slice(b * QB, (b + 1) * QB)
        p = e_own[:, sl].astype(F32) * fac[NG, :, sl]
        pb = p.astype(BF)
        ds = (p * (dp_own[:, sl] - fac[NG + 1, :, sl])).astype(BF)
        dv = dv + dot(pb, do[sl, :], NN)
        dk = dk + dot(ds, q[sl, :], NN)
    dck[...] = norm_back(ck_raw, kg, dk * SCALE).astype(BF)
    dcv[...] = dv.astype(BF)
    writes = [
        pltpu.make_async_copy(dck, dck_hbm, io_s.at[2]),
        pltpu.make_async_copy(dcv, dcv_hbm, io_s.at[3]),
    ]
    for w in writes:
        w.start()

    copy_o.wait_recv()
    for h in range(QH):
        sl = slice(h * TOK, (h + 1) * TOK)
        x = (ok_t[0:DH, sl] + o_rem[:, sl]).T
        out[:, h * DH : (h + 1) * DH] = jnp.where(live_rows, x, 0.0).astype(BF)
    write_o = pltpu.make_async_copy(out, out_hbm, io_s.at[4])
    write_o.start()

    g_start(2, g_wait(1))
    copy_ry(2).wait_recv()
    for i in range(4, 8):
        copy_rz(i).wait_recv()
    acc2 = part[1, 2 * OWN :, :] + y_in[2].astype(F32)
    far = z_in[6].astype(F32)
    up2 = acc2[0:OWN] + z_in[4].astype(F32)
    down2 = acc2[OWN:] + z_in[5].astype(F32)
    z_out[2, 0:HALF, :] = (up2[0:HALF] + far[0:HALF]).astype(BF)
    z_out[2, HALF:, :] = up2[HALF:].astype(BF)
    z_out[3, 0:HALF, :] = down2[0:HALF].astype(BF)
    z_out[3, HALF:, :] = (down2[HALF:] + far[HALF:]).astype(BF)
    copy_rz(2).start()
    copy_rz(3).start()

    copy_dq.wait_recv()
    for h in range(QH):
        sl = slice(h * TOK, (h + 1) * TOK)
        up = (dq_t[:, sl] + dq_rem[:, sl]).T * SCALE
        x = cq[:, h * DH : (h + 1) * DH].astype(F32)
        dq[:, h * DH : (h + 1) * DH] = norm_back(x, qg, up).astype(BF)
    write_dq = pltpu.make_async_copy(dq, dq_hbm, io_s.at[5])
    write_dq.start()

    copy_ry0.wait_recv()
    for i in range(4):
        copy_rz(i).wait_recv()
    total = part[0, 0:OWN, :] + y_in[0, OWN:, :].astype(F32)
    for i in range(4):
        total = total + z_in[i].astype(F32)
    dpk[...] = norm_back(pk_raw, kg, total[:, 0:DH] * SCALE).astype(BF)
    dpv[...] = total[:, DH:].astype(BF)
    write_pk = pltpu.make_async_copy(dpk, dpk_hbm, io_s.at[6])
    write_pv = pltpu.make_async_copy(dpv, dpv_hbm, io_s.at[7])
    write_pk.start()
    write_pv.start()

    g_sum = jnp.sum(g_wait(2), axis=0, keepdims=True) * (SCALE / math.sqrt(GAIN_ROWS))
    gains[0:1, :] = g_sum / qg
    gains[1:2, :] = g_sum / kg
    write_g = pltpu.make_async_copy(gains, gains_hbm, io_s.at[8])
    write_g.start()

    for i in range(8):
        copy_z(i).wait_send()
        copy_y(i).wait_send()
        copy_rz(i).wait_send()
    for c in (copy_q, copy_do, copy_st, copy_o, copy_dq, copy_ry0, copy_ry4):
        c.wait_send()
    for g in range(1, NG):
        copy_ry(g).wait_send()
    for r in range(3):
        for k in range(1, 8):
            j = lax.rem(my_slot[r] + k, 8)
            send(
                g_buf.at[r, my_slot[r]], g_buf.at[r, my_slot[r]], g_s.at[r, k], g_r.at[r, j], partner(r, j)
            ).wait_send()
    for w in writes + [write_o, write_dq, write_pk, write_pv, write_g]:
        w.wait()


def place(*refs):
    count = (len(refs) - 1) // 3
    src, dst, held, sems = refs[:count], refs[count : 2 * count], refs[2 * count : 3 * count], refs[-1]
    reads = [pltpu.make_async_copy(src[i], held[i], sems.at[0, i]) for i in range(count)]
    writes = [pltpu.make_async_copy(held[i], dst[i], sems.at[1, i]) for i in range(count)]
    for r in reads:
        r.start()
    for r, w in zip(reads, writes):
        r.wait()
        w.start()
    for w in writes:
        w.wait()


GAIN_ROWS = 524288


def per_device(comp_q, comp_k, comp_v, prompt_k, prompt_v, lengths, q_gain, k_gain, d_out):
    vmem = pl.BlockSpec(memory_space=pltpu.VMEM)
    smem = pl.BlockSpec(memory_space=pltpu.SMEM)
    dma = pltpu.SemaphoreType.DMA
    width = QH * DH
    shapes = [
        jax.ShapeDtypeStruct((TOK, width), BF),
        jax.ShapeDtypeStruct((TOK, width), BF),
        jax.ShapeDtypeStruct((TOK, DH), BF),
        jax.ShapeDtypeStruct((TOK, DH), BF),
        jax.ShapeDtypeStruct((OWN, DH), BF),
        jax.ShapeDtypeStruct((OWN, DH), BF),
        jax.ShapeDtypeStruct((2, DH), F32),
    ]
    scratch = [
        pltpu.VMEM((TOK, width), BF),
        pltpu.VMEM((TOK, width), BF),
        pltpu.VMEM((TOK, width), BF),
        pltpu.VMEM((TOK, width), BF),
        pltpu.VMEM((TOK, DH), BF),
        pltpu.VMEM((TOK, DH), BF),
        pltpu.VMEM((OWN, DH), BF),
        pltpu.VMEM((OWN, DH), BF),
        pltpu.VMEM((2, DH), F32),
        pltpu.VMEM((KEYS, 2 * DH), BF),
        pltpu.VMEM((Q2, DH), BF),
        pltpu.VMEM((Q2, DH), BF),
        pltpu.VMEM((TOK, 2 * DH), BF),
        pltpu.VMEM((2 * DH, GR), BF),
        pltpu.VMEM((GR, Q2), F32),
        pltpu.VMEM((KEYS, Q2), BF),
        pltpu.VMEM((GR, Q2), BF),
        pltpu.VMEM((KEYS, Q2), F32),
        pltpu.VMEM((TOK, NQ), BF),
        pltpu.VMEM((TOK, NQ), F32),
        pltpu.VMEM((2 * DH, Q2), F32),
        pltpu.VMEM((DH, Q2), F32),
        pltpu.VMEM((DH, NQ), F32),
        pltpu.VMEM((DH, NQ), F32),
        pltpu.VMEM((1, Q2), F32),
        pltpu.VMEM((NG + 1, 1, Q2), F32),
        pltpu.VMEM((8, Q2), F32),
        pltpu.VMEM((8, Q2), F32),
        pltpu.VMEM((NG + 2, 1, Q2), F32),
        pltpu.VMEM((NG, GR, 2 * DH), F32),
        pltpu.VMEM((NG, 2 * OWN, 2 * DH), BF),
        pltpu.VMEM((NG, 2 * OWN, 2 * DH), BF),
        pltpu.VMEM((OWN, 2 * DH), BF),
        pltpu.VMEM((OWN, 2 * DH), BF),
        pltpu.VMEM((7, OWN, 2 * DH), BF),
        pltpu.VMEM((7, OWN, 2 * DH), BF),
        pltpu.VMEM((3, 8, 8, DH), F32),
        dma((9,)), dma((8,)), dma((8,)), dma((8,)), dma((8,)), dma((5,)), dma((5,)),
        dma((5,)), dma((5,)), dma((8,)), dma((8,)), dma((3, 8)), dma((3, 8)),
    ]
    anywhere = pl.BlockSpec(memory_space=pl.ANY)
    res = pl.pallas_call(
        kernel,
        out_shape=shapes,
        in_specs=[anywhere] + [vmem] * 4 + [smem] + [vmem] * 2 + [anywhere],
        out_specs=[anywhere] * 7,
        scratch_shapes=scratch,
        compiler_params=pltpu.CompilerParams(
            collective_id=0, has_side_effects=True, vmem_limit_bytes=56 * 2**20
        ),
    )(
        comp_q.reshape(TOK, width),
        comp_k.reshape(TOK, DH),
        comp_v.reshape(TOK, DH),
        prompt_k.reshape(OWN, DH),
        prompt_v.reshape(OWN, DH),
        lengths,
        q_gain.reshape(1, DH),
        k_gain.reshape(1, DH),
        d_out.reshape(TOK, width),
    )
    res = pl.pallas_call(
        place,
        out_shape=shapes,
        in_specs=[anywhere] * 7,
        out_specs=[anywhere] * 7,
        scratch_shapes=[pltpu.VMEM(x.shape, x.dtype) for x in shapes] + [dma((2, 7))],
    )(*res)
    return (
        res[0].reshape(1, 1, TOK, width),
        res[1].reshape(1, 1, TOK, width),
        res[2].reshape(1, 1, TOK, DH),
        res[3].reshape(1, 1, TOK, DH),
        res[4].reshape(1, OWN, DH),
        res[5].reshape(1, OWN, DH),
        res[6],
    )


def solution(mesh):
    return jax.shard_map(
        per_device,
        mesh=mesh,
        in_specs=(
            P("prompt", "sample", None, "head"),
            P("prompt", "sample", None, "head"),
            P("prompt", "sample", None, "head"),
            P("prompt", "sample", "head"),
            P("prompt", "sample", "head"),
            P("prompt", "sample"),
            P(),
            P(),
            P("prompt", "sample", None, "head"),
        ),
        out_specs=(
            P("prompt", "sample", None, "head"),
            P("prompt", "sample", None, "head"),
            P("prompt", "sample", None, "head"),
            P("prompt", "sample", None, "head"),
            P("prompt", "sample", "head"),
            P("prompt", "sample", "head"),
            P(),
        ),
        check_vma=False,
    )
```

```python
import functools
import math

import jax
import jax.numpy as jnp
from jax import lax
from jax.experimental import pallas as pl
from jax.experimental.pallas import tpu as pltpu
from jax.sharding import PartitionSpec as P

EPS = 1e-06
BF = jnp.bfloat16
F32 = jnp.float32
NT = (((1,), (1,)), ((), ()))
NN = (((1,), (0,)), ((), ()))
DH = 128
TOK = 128
QH = 8
NQ = TOK * QH
Q2 = 2 * NQ
OWN = 96
GR = 4 * OWN
NG = 4
KEYS = NG * GR
QB = 256
SCALE = 1.0 / math.sqrt(DH)
C2 = SCALE / math.log(2.0)
LOW = -1e30
MESH = pl.DeviceIdType.MESH


def dot(a, b, dims):
    return lax.dot_general(a, b, dims, preferred_element_type=F32)


def rms(x):
    return lax.rsqrt(jnp.mean(x * x, axis=-1, keepdims=True) + EPS)


def norm_back(x, gain, up):
    r = rms(x)
    g = up * gain
    return r * g - x * (r * r * r * jnp.mean(x * g, axis=-1, keepdims=True))


def row_near(d):
    return ((d - 1) * 4 + 2) * OWN


def row_far(d):
    return (8, 4, 12)[d - 1] * OWN


ROW_FAR0 = OWN
ROW_FAR4 = (3 * 4 + 3) * OWN
HALF = OWN // 2


def kernel(
    cq_hbm, ck, cv, pk, pv, live_ref, q_gain, k_gain, dout_hbm,
    out_hbm, dq_hbm, dck_hbm, dcv_hbm, dpk_hbm, dpv_hbm, gains_hbm,
    cq, d_out, out, dq, dck, dcv, dpk, dpv, gains,
    kv, q, do, ownkv, trans, s_buf, e_buf, f_buf, dp_buf, e_own, dp_own, ok_t, dq_t, o_rem, dq_rem, m_run,
    m_at, stat, stat_rem, fac, part, y_out, y_in, z_out, z_in, g_buf,
    io_s, za_s, za_r, y_s, y_r, c_s, c_r, ry_s, ry_r, rz_s, rz_r, g_s, g_r,
):
    read_q = pltpu.make_async_copy(cq_hbm, cq, io_s.at[0])
    read_d = pltpu.make_async_copy(dout_hbm, d_out, io_s.at[1])
    read_q.start()
    read_d.start()

    sample = lax.axis_index("sample")
    px = lax.axis_index("prompt")
    hy = lax.axis_index("head")
    core = lax.rem(sample, 2)
    y = lax.rem(sample // 2, 2)
    z = sample // 4

    def at(z_, y_, c_):
        return z_ * 4 + y_ * 2 + c_

    sib = {"sample": at(z, y, 1 - core)}
    ynb = {"sample": at(z, 1 - y, core)}

    def z_dev(d):
        return {"sample": at(lax.rem(z + d + 8, 8), y, core)}

    my_slot = (px * 2 + core, z, hy * 2 + y)

    def partner(r, i):
        if r == 0:
            return {"prompt": i // 2, "sample": at(z, y, lax.rem(i, 2))}
        if r == 1:
            return {"sample": at(i, y, core)}
        return {"head": i // 2, "sample": at(z, lax.rem(i, 2), core)}

    def send(src, dst, ss, rs, dev):
        return pltpu.make_async_remote_copy(
            src_ref=src, dst_ref=dst, send_sem=ss, recv_sem=rs, device_id=dev, device_id_type=MESH
        )

    barrier = pltpu.get_barrier_semaphore()
    for r in (1, 2, 0):
        for k in range(1, 8):
            pl.semaphore_signal(
                barrier, inc=1, device_id=partner(r, lax.rem(my_slot[r] + k, 8)), device_id_type=MESH
            )

    kg = k_gain[...]
    qg = q_gain[...]
    pk_raw = pk[...].astype(F32)
    kv[0:OWN, 0:DH] = (pk_raw * rms(pk_raw) * kg).astype(BF)
    kv[0:OWN, DH:] = pv[...]
    pl.semaphore_wait(barrier, 21)

    def rows(start, count=OWN):
        return kv.at[pl.ds(start, count), :]

    def halves(to, dst, src):
        return [(to, dst, src), (to, dst + HALF, src + HALF)]

    z_plan = (
        halves(-1, row_near(1), 0)
        + halves(1, row_near(1) + OWN, 0)
        + halves(-2, row_near(2), 0)
        + halves(2, row_near(2) + OWN, 0)
        + halves(-1, row_near(3), row_near(2))
        + halves(1, row_near(3) + OWN, row_near(2) + OWN)
        + [(-2, row_near(4), row_near(2)), (2, row_near(4) + HALF, row_near(2) + OWN + HALF)]
        + halves(-2, row_far(2), ROW_FAR0)
        + halves(2, row_far(2) + OWN, ROW_FAR0)
        + halves(-1, row_far(3), row_far(2))
        + halves(1, row_far(3) + OWN, row_far(2) + OWN)
        + [(-2, ROW_FAR4, row_far(2)), (2, ROW_FAR4 + HALF, row_far(2) + OWN + HALF)]
    )

    def copy_z(i):
        to, dst, src = z_plan[i]
        return send(rows(src, HALF), rows(dst, HALF), za_s.at[i], za_r.at[i], z_dev(to))

    y_plan = [
        (dst + h, src + h)
        for dst, src in (
            (ROW_FAR0, 0),
            (row_far(1), row_near(1)),
            (row_far(1) + OWN, row_near(1) + OWN),
        )
        for h in (0, HALF)
    ]

    def copy_y(i):
        dst, src = y_plan[i]
        return send(rows(src, HALF), rows(dst, HALF), y_s.at[i], y_r.at[i], ynb)

    for i in (4, 6, 5, 7, 0, 2, 1, 3):
        copy_z(i).start()
    copy_y(0).start()
    copy_y(1).start()

    live_rows = lax.broadcasted_iota(jnp.int32, (TOK, 1), 0) < live_ref[...]
    read_q.wait()
    for h in range(QH):
        x = cq[:, h * DH : (h + 1) * DH].astype(F32)
        q[h * TOK : (h + 1) * TOK, :] = (x * rms(x) * qg).astype(BF)
    copy_q = send(q.at[0:NQ, :], q.at[NQ:, :], c_s.at[0], c_r.at[0], sib)
    copy_q.start()
    read_d.wait()
    for h in range(QH):
        g = d_out[:, h * DH : (h + 1) * DH]
        do[h * TOK : (h + 1) * TOK, :] = jnp.where(live_rows, g, jnp.zeros_like(g))
    copy_do = send(do.at[0:NQ, :], do.at[NQ:, :], c_s.at[1], c_r.at[1], sib)
    copy_do.start()

    ck_raw = ck[...].astype(F32)
    ownkv[:, 0:DH] = (ck_raw * rms(ck_raw) * kg).astype(BF)
    ownkv[:, DH:] = cv[...]

    def turn(keys, vals, count):
        trans[0:DH, 0:count] = vals.astype(F32).T.astype(BF)
        trans[DH:, 0:count] = keys.astype(F32).T.astype(BF)

    m_run[...] = jnp.full((1, Q2), LOW, F32)
    stat[...] = jnp.zeros((8, Q2), F32)
    ok_t[:, NQ:] = jnp.zeros((2 * DH, NQ), F32)
    dq_t[:, NQ:] = jnp.zeros((DH, NQ), F32)
    turn(ownkv[:, 0:DH], ownkv[:, DH:], TOK)
    u_ids = lax.broadcasted_iota(jnp.int32, (TOK, QB), 0)
    t_ids = lax.rem(lax.broadcasted_iota(jnp.int32, (TOK, QB), 1), TOK)
    allowed = u_ids <= t_ids
    for b in range(NQ // QB):
        sl = slice(b * QB, (b + 1) * QB)
        s = jnp.where(allowed, dot(ownkv[:, 0:DH], q[sl, :], NT), LOW)
        dp = dot(ownkv[:, DH:], do[sl, :], NT)
        m = jnp.max(s, axis=0, keepdims=True)
        e = jnp.exp2((s - m) * C2)
        eb = e.astype(BF)
        ed = e * dp
        e_own[:, sl] = eb
        dp_own[:, sl] = dp
        m_run[:, sl] = m
        stat[1:2, sl] = jnp.sum(e, axis=0, keepdims=True)
        stat[2:3, sl] = jnp.sum(ed, axis=0, keepdims=True)
        ok_t[:, sl] = dot(trans[:, 0:TOK], eb, NN)
        dq_t[:, sl] = dot(trans[DH:, 0:TOK], ed.astype(BF), NN)
    m_at[NG] = m_run[...]

    for h in range(2):
        copy_y(h).wait_recv()
        copy_z(14 + h).start()
        copy_z(16 + h).start()
    for h in range(2):
        copy_z(4 + h).wait_recv()
        copy_z(6 + h).wait_recv()
        for i in (8 + h, 12 + h, 10 + h):
            copy_z(i).start()
    for h in range(2):
        copy_z(h).wait_recv()
        copy_z(2 + h).wait_recv()
        copy_y(2 + h).start()
        copy_y(4 + h).start()
    copy_q.wait_recv()
    copy_do.wait_recv()

    tiles = Q2 // QB

    def tile(b):
        return slice(b * QB, (b + 1) * QB)

    def rise(b, mx):
        m_old = m_run[:, tile(b)]
        m_new = jnp.maximum(m_old, mx)
        m_run[:, tile(b)] = m_new
        return jnp.exp2((m_old - m_new) * C2), m_new * C2

    def scores(b, at_rows, keys, vals):
        s = dot(keys, q[tile(b), :], NT)
        s_buf[:, tile(b)] = s
        dp_buf[at_rows, tile(b)] = dot(vals, do[tile(b), :], NT)
        return jnp.max(s, axis=0, keepdims=True)

    def weigh(b, at_rows, al, mc):
        sl = tile(b)
        e = jnp.exp2(s_buf[:, sl] * C2 - mc)
        ed = e * dp_buf[at_rows, sl]
        e_buf[at_rows, sl] = e.astype(BF)
        f_buf[:, sl] = ed.astype(BF)
        stat[1:2, sl] = stat[1:2, sl] * al + jnp.sum(e, axis=0, keepdims=True)
        stat[2:3, sl] = stat[2:3, sl] * al + jnp.sum(ed, axis=0, keepdims=True)

    def mix(b, at_rows, al):
        sl = tile(b)
        ok_t[:, sl] = ok_t[:, sl] * al + dot(trans[...], e_buf[at_rows, sl], NN)
        dq_t[:, sl] = dq_t[:, sl] * al + dot(trans[DH:, :], f_buf[:, sl], NN)

    def forward(g, carry):
        @pl.when(g == 1)
        def _():
            for h in range(2):
                copy_z(14 + h).wait_recv()
                copy_z(16 + h).wait_recv()
                for j in (18 + h, 20 + h, 22 + h):
                    copy_z(j).start()

        @pl.when(g == 2)
        def _():
            for i in range(2, 6):
                copy_y(i).wait_recv()
            for i in range(8, 12):
                copy_z(i).wait_recv()

        at_rows = pl.ds(pl.multiple_of(g * GR, GR), GR)
        keys = kv[at_rows, 0:DH]
        vals = kv[at_rows, DH:]
        turn(keys, vals, GR)
        mx, al, mc = {}, {}, {}
        for t in range(tiles + 2):
            if 1 <= t <= tiles:
                al[t - 1], mc[t - 1] = rise(t - 1, mx[t - 1])
            if t < tiles:
                mx[t] = scores(t, at_rows, keys, vals)
            if 1 <= t <= tiles:
                weigh(t - 1, at_rows, al[t - 1], mc[t - 1])
            if t >= 2:
                mix(t - 2, at_rows, al[t - 2])
        m_at[g] = m_run[...]
        return carry

    lax.fori_loop(0, NG - 1, forward, 0)

    for i in (12, 13, 18, 19, 20, 21, 22, 23):
        copy_z(i).wait_recv()
    last = slice((NG - 1) * GR, NG * GR)
    keys = kv[last, 0:DH]
    vals = kv[last, DH:]
    mx, al, mc = {}, {}, {}
    for t in range(tiles + 1):
        if t >= 1:
            al[t - 1], mc[t - 1] = rise(t - 1, mx[t - 1])
        if t < tiles:
            mx[t] = scores(t, last, keys, vals)
        if t >= 1:
            weigh(t - 1, last, al[t - 1], mc[t - 1])
    m_at[NG - 1] = m_run[...]

    stat[0:1, :] = m_run[...]
    copy_st = send(stat, stat_rem, c_s.at[2], c_r.at[2], sib)
    copy_st.start()
    turn(keys, vals, GR)
    for b in range(tiles):
        mix(b, last, al[b])
    copy_st.wait_recv()
    for half in range(2):
        mine = slice(half * NQ, (half + 1) * NQ)
        other = slice((1 - half) * NQ, (2 - half) * NQ)
        m_a, m_b = stat[0:1, mine], stat_rem[0:1, other]
        m_f = jnp.maximum(m_a, m_b)
        w_a, w_b = jnp.exp2((m_a - m_f) * C2), jnp.exp2((m_b - m_f) * C2)
        inv = 1.0 / (stat[1:2, mine] * w_a + stat_rem[1:2, other] * w_b)
        for i in range(NG + (1 - half)):
            fac[i, :, mine] = jnp.exp2((m_at[i, :, mine] - m_f) * C2) * inv
        fac[NG + 1, :, mine] = (stat[2:3, mine] * w_a + stat_rem[2:3, other] * w_b) * inv
        fac[NG + 2, :, mine] = w_a * inv

    def g_start(r, value):
        g_buf[r, my_slot[r]] = value
        for k in range(1, 8):
            send(
                g_buf.at[r, my_slot[r]], g_buf.at[r, my_slot[r]], g_s.at[r, k], g_r.at[r, my_slot[r]],
                partner(r, lax.rem(my_slot[r] + k, 8)),
            ).start()

    def g_wait(r):
        for k in range(1, 8):
            j = lax.rem(my_slot[r] + k, 8)
            send(
                g_buf.at[r, j], g_buf.at[r, j], g_s.at[r, k], g_r.at[r, j], partner(r, j)
            ).wait_recv()
        total = g_buf[r, 0]
        for k in range(1, 8):
            total = total + g_buf[r, k]
        return total

    def copy_ry(g, h):
        at_rows = pl.ds(h * HALF, HALF)
        return [
            send(
                y_out.at[g, sign, at_rows], y_in.at[g, sign, at_rows],
                ry_s.at[g, sign, h], ry_r.at[g, sign, h], ynb,
            )
            for sign in range(2)
        ]

    def copy_ry4(h):
        at_rows = pl.ds(h * HALF, HALF)
        return send(
            y_out.at[1, 0, at_rows], y_in.at[1, 0, at_rows], ry_s.at[1, 0, h], ry_r.at[1, 0, h], ynb
        )

    copy_ry0 = send(y_out.at[0, 0], y_in.at[0, 0], ry_s.at[0, 0, 0], ry_r.at[0, 0, 0], ynb)

    rz_plan = [
        (to, slot, h)
        for slot, to in ((0, 1), (1, -1), (2, 2), (3, -2), (4, 1), (5, -1))
        for h in (0, HALF)
    ] + [(2, 6, 0), (-2, 6, HALF)]
    rz_plan += [(to, slot, h) for slot, to in ((7, 1), (8, -1)) for h in (0, HALF)]

    def copy_rz(i):
        to, slot, h = rz_plan[i]
        at_slot = (slot, pl.ds(h, HALF))
        return send(z_out.at[at_slot], z_in.at[at_slot], rz_s.at[i], rz_r.at[i], z_dev(to))

    def gradients(g, at_rows):
        dk = jnp.zeros((GR, DH), F32)
        dv = jnp.zeros((GR, DH), F32)
        for b in range(tiles):
            sl = tile(b)
            p = e_buf[at_rows, sl].astype(F32) * fac[g, :, sl]
            pb = p.astype(BF)
            ds = (p * (dp_buf[at_rows, sl] - fac[NG + 1, :, sl])).astype(BF)
            dv = dv + dot(pb, do[sl, :], NN)
            dk = dk + dot(ds, q[sl, :], NN)
        part[g, :, 0:DH] = dk
        part[g, :, DH:] = dv

    gradients(NG - 1, last)
    y_out[3, 0] = part[3, 0:OWN, :].astype(BF)
    y_out[3, 1] = part[3, OWN : 2 * OWN, :].astype(BF)
    y_out[1, 0] = part[3, 3 * OWN :, :].astype(BF)
    for h in range(2):
        for c in copy_ry(3, h):
            c.start()
        copy_ry4(h).start()

    own = fac[NG + 2]
    ok_t[0:DH, :] = ok_t[0:DH, :] * own
    dq_t[...] = (dq_t[...] - ok_t[DH:, :] * fac[NG + 1]) * own
    copy_dq = send(dq_t.at[:, NQ:], dq_rem, c_s.at[4], c_r.at[4], sib)
    copy_dq.start()
    copy_o = send(ok_t.at[0:DH, NQ:], o_rem, c_s.at[3], c_r.at[3], sib)
    copy_o.start()
    pairs = dot(dq_t[...].astype(BF), q[...], NN)
    eye = lax.broadcasted_iota(jnp.int32, (DH, DH), 0) == lax.broadcasted_iota(jnp.int32, (DH, DH), 1)
    g_start(0, jnp.sum(jnp.where(eye, pairs, 0.0).reshape(DH // 8, 8, DH), axis=0))

    def far_sums(h):
        for c in copy_ry(3, h):
            c.wait_recv()
        copy_ry4(h).wait_recv()
        r = slice(h * HALF, (h + 1) * HALF)
        for sign in range(2):
            start = (2 + sign) * OWN + h * HALF
            z_out[4 + sign, r, :] = (
                part[2, start : start + HALF, :] + y_in[3, sign, r, :].astype(F32)
            ).astype(BF)
            copy_rz(8 + 2 * sign + h).start()
        start = 2 * OWN + h * HALF
        z_out[6, r, :] = (part[3, start : start + HALF, :] + y_in[1, 0, r, :].astype(F32)).astype(BF)
        copy_rz(12 + h).start()

    def backward(i, carry):
        g = NG - 2 - i
        gradients(g, pl.ds(pl.multiple_of(g * GR, GR), GR))

        @pl.when(g == 2)
        def _():
            z_out[7] = part[2, 0:OWN, :].astype(BF)
            z_out[8] = part[2, OWN : 2 * OWN, :].astype(BF)
            for j in range(14, 18):
                copy_rz(j).start()

        @pl.when(g == 1)
        def _():
            y_out[2, 0] = part[1, 0:OWN, :].astype(BF)
            y_out[2, 1] = part[1, OWN : 2 * OWN, :].astype(BF)
            for h in range(2):
                for c in copy_ry(2, h):
                    c.start()
            far_sums(0)

        return carry

    lax.fori_loop(0, NG - 1, backward, 0)

    far_sums(1)
    z_out[0] = part[0, 2 * OWN : 3 * OWN, :].astype(BF)
    z_out[1] = part[0, 3 * OWN :, :].astype(BF)
    for j in range(4):
        copy_rz(j).start()
    g_start(1, g_wait(0))

    dk = jnp.zeros((TOK, DH), F32)
    dv = jnp.zeros((TOK, DH), F32)
    for b in range(NQ // QB):
        sl = slice(b * QB, (b + 1) * QB)
        p = e_own[:, sl].astype(F32) * fac[NG, :, sl]
        pb = p.astype(BF)
        ds = (p * (dp_own[:, sl] - fac[NG + 1, :, sl])).astype(BF)
        dv = dv + dot(pb, do[sl, :], NN)
        dk = dk + dot(ds, q[sl, :], NN)
    dck[...] = norm_back(ck_raw, kg, dk * SCALE).astype(BF)
    dcv[...] = dv.astype(BF)
    writes = [
        pltpu.make_async_copy(dck, dck_hbm, io_s.at[2]),
        pltpu.make_async_copy(dcv, dcv_hbm, io_s.at[3]),
    ]
    for w in writes:
        w.start()

    copy_o.wait_recv()
    for h in range(QH):
        sl = slice(h * TOK, (h + 1) * TOK)
        x = (ok_t[0:DH, sl] + o_rem[:, sl]).T
        out[:, h * DH : (h + 1) * DH] = jnp.where(live_rows, x, 0.0).astype(BF)
    write_o = pltpu.make_async_copy(out, out_hbm, io_s.at[4])
    write_o.start()

    g_start(2, g_wait(1))
    for j in range(14, 18):
        copy_rz(j).wait_recv()
    y_out[0, 0] = (
        part[0, OWN : 2 * OWN, :] + z_in[7].astype(F32) + z_in[8].astype(F32)
    ).astype(BF)
    copy_ry0.start()
    for h in range(2):
        for c in copy_ry(2, h):
            c.wait_recv()
        copy_rz(8 + h).wait_recv()
        copy_rz(10 + h).wait_recv()
        copy_rz(12 + h).wait_recv()
        r = slice(h * HALF, (h + 1) * HALF)
        for sign in range(2):
            start = (2 + sign) * OWN + h * HALF
            acc = part[1, start : start + HALF, :] + y_in[2, sign, r, :].astype(F32)
            acc = acc + z_in[4 + sign, r, :].astype(F32)
            if sign == h:
                acc = acc + z_in[6, r, :].astype(F32)
            z_out[2 + sign, r, :] = acc.astype(BF)
            copy_rz(4 + 2 * sign + h).start()

    copy_dq.wait_recv()
    for h in range(QH):
        sl = slice(h * TOK, (h + 1) * TOK)
        up = (dq_t[:, sl] + dq_rem[:, sl]).T * SCALE
        x = cq[:, h * DH : (h + 1) * DH].astype(F32)
        dq[:, h * DH : (h + 1) * DH] = norm_back(x, qg, up).astype(BF)
    write_dq = pltpu.make_async_copy(dq, dq_hbm, io_s.at[5])
    write_dq.start()

    copy_ry0.wait_recv()
    for j in range(8):
        copy_rz(j).wait_recv()
    total = part[0, 0:OWN, :] + y_in[0, 0].astype(F32)
    for i in range(4):
        total = total + z_in[i].astype(F32)
    dpk[...] = norm_back(pk_raw, kg, total[:, 0:DH] * SCALE).astype(BF)
    dpv[...] = total[:, DH:].astype(BF)
    write_pk = pltpu.make_async_copy(dpk, dpk_hbm, io_s.at[6])
    write_pv = pltpu.make_async_copy(dpv, dpv_hbm, io_s.at[7])
    write_pk.start()
    write_pv.start()

    g_sum = jnp.sum(g_wait(2), axis=0, keepdims=True) * (SCALE / math.sqrt(GAIN_ROWS))
    gains[0:1, :] = g_sum / qg
    gains[1:2, :] = g_sum / kg
    write_g = pltpu.make_async_copy(gains, gains_hbm, io_s.at[8])
    write_g.start()

    for i in range(24):
        copy_z(i).wait_send()
    for i in range(18):
        copy_rz(i).wait_send()
    for i in range(6):
        copy_y(i).wait_send()
    for c in (copy_q, copy_do, copy_st, copy_o, copy_dq, copy_ry0):
        c.wait_send()
    for h in range(2):
        copy_ry4(h).wait_send()
        for c in copy_ry(2, h) + copy_ry(3, h):
            c.wait_send()
    for r in range(3):
        for k in range(1, 8):
            j = lax.rem(my_slot[r] + k, 8)
            send(
                g_buf.at[r, my_slot[r]], g_buf.at[r, my_slot[r]], g_s.at[r, k], g_r.at[r, j], partner(r, j)
            ).wait_send()
    for w in writes + [write_o, write_dq, write_pk, write_pv, write_g]:
        w.wait()


def place(*refs):
    count = (len(refs) - 1) // 3
    src, dst, held, sems = refs[:count], refs[count : 2 * count], refs[2 * count : 3 * count], refs[-1]
    reads = [pltpu.make_async_copy(src[i], held[i], sems.at[0, i]) for i in range(count)]
    writes = [pltpu.make_async_copy(held[i], dst[i], sems.at[1, i]) for i in range(count)]
    for r in reads:
        r.start()
    for r, w in zip(reads, writes):
        r.wait()
        w.start()
    for w in writes:
        w.wait()


GAIN_ROWS = 524288


def per_device(comp_q, comp_k, comp_v, prompt_k, prompt_v, lengths, q_gain, k_gain, d_out):
    vmem = pl.BlockSpec(memory_space=pltpu.VMEM)
    dma = pltpu.SemaphoreType.DMA
    width = QH * DH
    shapes = [
        jax.ShapeDtypeStruct((TOK, width), BF),
        jax.ShapeDtypeStruct((TOK, width), BF),
        jax.ShapeDtypeStruct((TOK, DH), BF),
        jax.ShapeDtypeStruct((TOK, DH), BF),
        jax.ShapeDtypeStruct((OWN, DH), BF),
        jax.ShapeDtypeStruct((OWN, DH), BF),
        jax.ShapeDtypeStruct((2, DH), F32),
    ]
    scratch = [
        pltpu.VMEM((TOK, width), BF),
        pltpu.VMEM((TOK, width), BF),
        pltpu.VMEM((TOK, width), BF),
        pltpu.VMEM((TOK, width), BF),
        pltpu.VMEM((TOK, DH), BF),
        pltpu.VMEM((TOK, DH), BF),
        pltpu.VMEM((OWN, DH), BF),
        pltpu.VMEM((OWN, DH), BF),
        pltpu.VMEM((2, DH), F32),
        pltpu.VMEM((KEYS, 2 * DH), BF),
        pltpu.VMEM((Q2, DH), BF),
        pltpu.VMEM((Q2, DH), BF),
        pltpu.VMEM((TOK, 2 * DH), BF),
        pltpu.VMEM((2 * DH, GR), BF),
        pltpu.VMEM((GR, Q2), F32),
        pltpu.VMEM((KEYS, Q2), BF),
        pltpu.VMEM((GR, Q2), BF),
        pltpu.VMEM((KEYS, Q2), F32),
        pltpu.VMEM((TOK, NQ), BF),
        pltpu.VMEM((TOK, NQ), F32),
        pltpu.VMEM((2 * DH, Q2), F32),
        pltpu.VMEM((DH, Q2), F32),
        pltpu.VMEM((DH, NQ), F32),
        pltpu.VMEM((DH, NQ), F32),
        pltpu.VMEM((1, Q2), F32),
        pltpu.VMEM((NG + 1, 1, Q2), F32),
        pltpu.VMEM((8, Q2), F32),
        pltpu.VMEM((8, Q2), F32),
        pltpu.VMEM((NG + 3, 1, Q2), F32),
        pltpu.VMEM((NG, GR, 2 * DH), F32),
        pltpu.VMEM((NG, 2, OWN, 2 * DH), BF),
        pltpu.VMEM((NG, 2, OWN, 2 * DH), BF),
        pltpu.VMEM((9, OWN, 2 * DH), BF),
        pltpu.VMEM((9, OWN, 2 * DH), BF),
        pltpu.VMEM((3, 8, 8, DH), F32),
        dma((9,)), dma((24,)), dma((24,)), dma((6,)), dma((6,)), dma((5,)), dma((5,)),
        dma((NG, 2, 2)), dma((NG, 2, 2)), dma((18,)), dma((18,)), dma((3, 8)), dma((3, 8)),
    ]
    anywhere = pl.BlockSpec(memory_space=pl.ANY)
    res = pl.pallas_call(
        kernel,
        out_shape=shapes,
        in_specs=[anywhere] + [vmem] * 7 + [anywhere],
        out_specs=[anywhere] * 7,
        scratch_shapes=scratch,
        compiler_params=pltpu.CompilerParams(
            collective_id=0, has_side_effects=True, vmem_limit_bytes=56 * 2**20
        ),
    )(
        comp_q.reshape(TOK, width),
        comp_k.reshape(TOK, DH),
        comp_v.reshape(TOK, DH),
        prompt_k.reshape(OWN, DH),
        prompt_v.reshape(OWN, DH),
        lengths,
        q_gain.reshape(1, DH),
        k_gain.reshape(1, DH),
        d_out.reshape(TOK, width),
    )
    res = pl.pallas_call(
        place,
        out_shape=shapes,
        in_specs=[anywhere] * 7,
        out_specs=[anywhere] * 7,
        scratch_shapes=[pltpu.VMEM(x.shape, x.dtype) for x in shapes] + [dma((2, 7))],
    )(*res)
    return (
        res[0].reshape(1, 1, TOK, width),
        res[1].reshape(1, 1, TOK, width),
        res[2].reshape(1, 1, TOK, DH),
        res[3].reshape(1, 1, TOK, DH),
        res[4].reshape(1, OWN, DH),
        res[5].reshape(1, OWN, DH),
        res[6],
    )


def solution(mesh):
    return jax.shard_map(
        per_device,
        mesh=mesh,
        in_specs=(
            P("prompt", "sample", None, "head"),
            P("prompt", "sample", None, "head"),
            P("prompt", "sample", None, "head"),
            P("prompt", "sample", "head"),
            P("prompt", "sample", "head"),
            P("prompt", "sample"),
            P(),
            P(),
            P("prompt", "sample", None, "head"),
        ),
        out_specs=(
            P("prompt", "sample", None, "head"),
            P("prompt", "sample", None, "head"),
            P("prompt", "sample", None, "head"),
            P("prompt", "sample", None, "head"),
            P("prompt", "sample", "head"),
            P("prompt", "sample", "head"),
            P(),
        ),
        check_vma=False,
    )
```

```python
import functools
import math

import jax
import jax.numpy as jnp
from jax import lax
from jax.experimental import pallas as pl
from jax.experimental.pallas import tpu as pltpu
from jax.sharding import PartitionSpec as P

EPS = 1e-06
BF = jnp.bfloat16
F32 = jnp.float32
NT = (((1,), (1,)), ((), ()))
NN = (((1,), (0,)), ((), ()))
DH = 128
TOK = 128
QH = 8
NQ = TOK * QH
Q2 = 2 * NQ
OWN = 96
GR = 4 * OWN
NG = 4
KEYS = NG * GR
QB = 256
SCALE = 1.0 / math.sqrt(DH)
C2 = SCALE / math.log(2.0)
LOW = -1e30
MESH = pl.DeviceIdType.MESH


def dot(a, b, dims):
    return lax.dot_general(a, b, dims, preferred_element_type=F32)


def rms(x):
    return lax.rsqrt(jnp.mean(x * x, axis=-1, keepdims=True) + EPS)


def norm_back(x, gain, up):
    r = rms(x)
    g = up * gain
    return r * g - x * (r * r * r * jnp.mean(x * g, axis=-1, keepdims=True))


def row_near(d):
    return ((d - 1) * 4 + 2) * OWN


def row_far(d):
    return (8, 4, 12)[d - 1] * OWN


ROW_FAR0 = OWN
ROW_FAR4 = (3 * 4 + 3) * OWN
HALF = OWN // 2


def kernel(
    cq_hbm, ck_hbm, cv_hbm, pk_hbm, pv_hbm, live_hbm, q_gain_hbm, k_gain_hbm, dout_hbm,
    out_hbm, dq_hbm, dck_hbm, dcv_hbm, dpk_hbm, dpv_hbm, gains_hbm,
    cq, ck, cv, pk, pv, live_ref, q_gain, k_gain, d_out, out, dq, dck, dcv, dpk, dpv, gains,
    kv, q, do, ownkv, trans, trans_half, trans_own, s_buf, e_buf, f_buf, dp_buf, e_own, dp_own, ok_t, dq_t, o_rem, dq_rem, m_run,
    m_at, stat, stat_rem, fac, part, y_out, y_in, z_out, z_in, g_buf,
    io_s, za_s, za_r, y_s, y_r, c_s, c_r, ry_s, ry_r, rz_s, rz_r, g_s, g_r,
):
    reads = [
        pltpu.make_async_copy(src, dst, io_s.at[9 + i])
        for i, (src, dst) in enumerate(
            (
                (pk_hbm, pk), (k_gain_hbm, k_gain), (pv_hbm, pv), (cq_hbm, cq), (q_gain_hbm, q_gain),
                (live_hbm, live_ref), (dout_hbm, d_out), (ck_hbm, ck), (cv_hbm, cv),
            )
        )
    ]
    for r in reads:
        r.start()

    sample = lax.axis_index("sample")
    px = lax.axis_index("prompt")
    hy = lax.axis_index("head")
    core = lax.rem(sample, 2)
    y = lax.rem(sample // 2, 2)
    z = sample // 4

    def at(z_, y_, c_):
        return z_ * 4 + y_ * 2 + c_

    sib = {"sample": at(z, y, 1 - core)}
    ynb = {"sample": at(z, 1 - y, core)}

    def z_dev(d):
        return {"sample": at(lax.rem(z + d + 8, 8), y, core)}

    my_slot = (px * 2 + core, z, hy * 2 + y)

    def partner(r, i):
        if r == 0:
            return {"prompt": i // 2, "sample": at(z, y, lax.rem(i, 2))}
        if r == 1:
            return {"sample": at(i, y, core)}
        return {"head": i // 2, "sample": at(z, lax.rem(i, 2), core)}

    def send(src, dst, ss, rs, dev):
        return pltpu.make_async_remote_copy(
            src_ref=src, dst_ref=dst, send_sem=ss, recv_sem=rs, device_id=dev, device_id_type=MESH
        )

    barrier = pltpu.get_barrier_semaphore()
    for r in (1, 2, 0):
        for k in range(1, 8):
            pl.semaphore_signal(
                barrier, inc=1, device_id=partner(r, lax.rem(my_slot[r] + k, 8)), device_id_type=MESH
            )

    for r in reads[0:3]:
        r.wait()
    kg = k_gain[...]
    pk_raw = pk[...].astype(F32)
    kv[0:OWN, 0:DH] = (pk_raw * rms(pk_raw) * kg).astype(BF)
    kv[0:OWN, DH:] = pv[...]
    pl.semaphore_wait(barrier, 21)

    def rows(start, count=OWN):
        return kv.at[pl.ds(start, count), :]

    def halves(to, dst, src):
        return [(to, dst, src), (to, dst + HALF, src + HALF)]

    z_plan = (
        halves(-1, row_near(1), 0)
        + halves(1, row_near(1) + OWN, 0)
        + halves(-2, row_near(2), 0)
        + halves(2, row_near(2) + OWN, 0)
        + halves(-1, row_near(3), row_near(2))
        + halves(1, row_near(3) + OWN, row_near(2) + OWN)
        + [(-2, row_near(4), row_near(2)), (2, row_near(4) + HALF, row_near(2) + OWN + HALF)]
        + halves(-2, row_far(2), ROW_FAR0)
        + halves(2, row_far(2) + OWN, ROW_FAR0)
        + halves(-1, row_far(3), row_far(2))
        + halves(1, row_far(3) + OWN, row_far(2) + OWN)
        + [(-2, ROW_FAR4, row_far(2)), (2, ROW_FAR4 + HALF, row_far(2) + OWN + HALF)]
    )

    def copy_z(i):
        to, dst, src = z_plan[i]
        return send(rows(src, HALF), rows(dst, HALF), za_s.at[i], za_r.at[i], z_dev(to))

    y_plan = [
        (dst + h, src + h)
        for dst, src in (
            (ROW_FAR0, 0),
            (row_far(1), row_near(1)),
            (row_far(1) + OWN, row_near(1) + OWN),
        )
        for h in (0, HALF)
    ]

    def copy_y(i):
        dst, src = y_plan[i]
        return send(rows(src, HALF), rows(dst, HALF), y_s.at[i], y_r.at[i], ynb)

    for i in (4, 6, 5, 7, 0, 2, 1, 3):
        copy_z(i).start()
    copy_y(0).start()
    copy_y(1).start()

    for r in reads[3:6]:
        r.wait()
    qg = q_gain[...]
    live_rows = lax.broadcasted_iota(jnp.int32, (TOK, 1), 0) < live_ref[...]
    for h in range(QH):
        x = cq[:, h * DH : (h + 1) * DH].astype(F32)
        q[h * TOK : (h + 1) * TOK, :] = (x * rms(x) * qg).astype(BF)
    copy_q = send(q.at[0:NQ, :], q.at[NQ:, :], c_s.at[0], c_r.at[0], sib)
    copy_q.start()
    reads[6].wait()
    for h in range(QH):
        g = d_out[:, h * DH : (h + 1) * DH]
        do[h * TOK : (h + 1) * TOK, :] = jnp.where(live_rows, g, jnp.zeros_like(g))
    copy_do = send(do.at[0:NQ, :], do.at[NQ:, :], c_s.at[1], c_r.at[1], sib)
    copy_do.start()

    reads[7].wait()
    reads[8].wait()
    ck_raw = ck[...].astype(F32)
    ownkv[:, 0:DH] = (ck_raw * rms(ck_raw) * kg).astype(BF)
    ownkv[:, DH:] = cv[...]

    def turn(keys, vals, into):
        into[0:DH, :] = vals.astype(F32).T.astype(BF)
        into[DH:, :] = keys.astype(F32).T.astype(BF)

    m_run[...] = jnp.full((1, Q2), LOW, F32)
    stat[...] = jnp.zeros((8, Q2), F32)
    ok_t[:, NQ:] = jnp.zeros((2 * DH, NQ), F32)
    dq_t[:, NQ:] = jnp.zeros((DH, NQ), F32)
    turn(ownkv[:, 0:DH], ownkv[:, DH:], trans_own)
    u_ids = lax.broadcasted_iota(jnp.int32, (TOK, QB), 0)
    t_ids = lax.rem(lax.broadcasted_iota(jnp.int32, (TOK, QB), 1), TOK)
    allowed = u_ids <= t_ids
    for b in range(NQ // QB):
        sl = slice(b * QB, (b + 1) * QB)
        s = jnp.where(allowed, dot(ownkv[:, 0:DH], q[sl, :], NT), LOW)
        dp = dot(ownkv[:, DH:], do[sl, :], NT)
        m = jnp.max(s, axis=0, keepdims=True)
        e = jnp.exp2((s - m) * C2)
        eb = e.astype(BF)
        ed = e * dp
        e_own[:, sl] = eb
        dp_own[:, sl] = dp
        m_run[:, sl] = m
        stat[1:2, sl] = jnp.sum(e, axis=0, keepdims=True)
        stat[2:3, sl] = jnp.sum(ed, axis=0, keepdims=True)
        ok_t[:, sl] = dot(trans_own[...], eb, NN)
        dq_t[:, sl] = dot(trans_own[DH:, :], ed.astype(BF), NN)
    m_at[NG] = m_run[...]

    for h in range(2):
        copy_y(h).wait_recv()
        copy_z(14 + h).start()
        copy_z(16 + h).start()
    copy_q.wait_recv()
    copy_do.wait_recv()

    tiles = Q2 // QB

    def tile(b):
        return slice(b * QB, (b + 1) * QB)

    def rise(b, mx):
        m_old = m_run[:, tile(b)]
        m_new = jnp.maximum(m_old, mx)
        m_run[:, tile(b)] = m_new
        return jnp.exp2((m_old - m_new) * C2), m_new * C2

    def scores(b, at_rows, keys, vals):
        s = dot(keys, q[tile(b), :], NT)
        s_buf[0 : keys.shape[0], tile(b)] = s
        dp_buf[at_rows, tile(b)] = dot(vals, do[tile(b), :], NT)
        return jnp.max(s, axis=0, keepdims=True)

    def weigh(b, at_rows, al, mc, count):
        sl = tile(b)
        e = jnp.exp2(s_buf[0:count, sl] * C2 - mc)
        ed = e * dp_buf[at_rows, sl]
        e_buf[at_rows, sl] = e.astype(BF)
        f_buf[0:count, sl] = ed.astype(BF)
        stat[1:2, sl] = stat[1:2, sl] * al + jnp.sum(e, axis=0, keepdims=True)
        stat[2:3, sl] = stat[2:3, sl] * al + jnp.sum(ed, axis=0, keepdims=True)

    def mix(b, at_rows, al, turned, count):
        sl = tile(b)
        ok_t[:, sl] = ok_t[:, sl] * al + dot(turned[...], e_buf[at_rows, sl], NN)
        dq_t[:, sl] = dq_t[:, sl] * al + dot(turned[DH:, :], f_buf[0:count, sl], NN)

    def attend(at_rows, turned, count):
        keys = kv[at_rows, 0:DH]
        vals = kv[at_rows, DH:]
        turn(keys, vals, turned)
        mx, al, mc = {}, {}, {}
        for t in range(tiles + 2):
            if 1 <= t <= tiles:
                al[t - 1], mc[t - 1] = rise(t - 1, mx[t - 1])
            if t < tiles:
                mx[t] = scores(t, at_rows, keys, vals)
            if 1 <= t <= tiles:
                weigh(t - 1, at_rows, al[t - 1], mc[t - 1], count)
            if t >= 2:
                mix(t - 2, at_rows, al[t - 2], turned, count)

    def forward_half(i, carry):
        @pl.when(i == 1)
        def _():
            for h in range(2):
                copy_z(4 + h).wait_recv()
                copy_z(6 + h).wait_recv()
                for i in (8 + h, 12 + h, 10 + h):
                    copy_z(i).start()
            for h in range(2):
                copy_z(h).wait_recv()
                copy_z(2 + h).wait_recv()
                copy_y(2 + h).start()
                copy_y(4 + h).start()

        attend(pl.ds(pl.multiple_of(i * (GR // 2), GR // 2), GR // 2), trans_half, GR // 2)
        m_at[i * (NG + 1)] = m_run[...]
        return carry

    lax.fori_loop(0, 2, forward_half, 0)

    def forward(g, carry):
        @pl.when(g == 1)
        def _():
            for h in range(2):
                copy_z(14 + h).wait_recv()
                copy_z(16 + h).wait_recv()
                for j in (18 + h, 20 + h, 22 + h):
                    copy_z(j).start()

        @pl.when(g == 2)
        def _():
            for i in range(2, 6):
                copy_y(i).wait_recv()
            for i in range(8, 12):
                copy_z(i).wait_recv()

        attend(pl.ds(pl.multiple_of(g * GR, GR), GR), trans, GR)
        m_at[g] = m_run[...]
        return carry

    lax.fori_loop(1, NG - 1, forward, 0)

    for i in (12, 13, 18, 19, 20, 21, 22, 23):
        copy_z(i).wait_recv()
    last = slice((NG - 1) * GR, NG * GR)
    keys = kv[last, 0:DH]
    vals = kv[last, DH:]
    mx, al, mc = {}, {}, {}
    for t in range(tiles + 1):
        if t >= 1:
            al[t - 1], mc[t - 1] = rise(t - 1, mx[t - 1])
        if t < tiles:
            mx[t] = scores(t, last, keys, vals)
        if t >= 1:
            weigh(t - 1, last, al[t - 1], mc[t - 1], GR)
    m_at[NG - 1] = m_run[...]

    stat[0:1, :] = m_run[...]
    copy_st = send(stat, stat_rem, c_s.at[2], c_r.at[2], sib)
    copy_st.start()
    turn(keys, vals, trans)
    for b in range(tiles):
        mix(b, last, al[b], trans, GR)
    copy_st.wait_recv()
    for half in range(2):
        mine = slice(half * NQ, (half + 1) * NQ)
        other = slice((1 - half) * NQ, (2 - half) * NQ)
        m_a, m_b = stat[0:1, mine], stat_rem[0:1, other]
        m_f = jnp.maximum(m_a, m_b)
        w_a, w_b = jnp.exp2((m_a - m_f) * C2), jnp.exp2((m_b - m_f) * C2)
        inv = 1.0 / (stat[1:2, mine] * w_a + stat_rem[1:2, other] * w_b)
        for i in range(NG + (1 - half)):
            fac[i, :, mine] = jnp.exp2((m_at[i, :, mine] - m_f) * C2) * inv
        fac[NG + 1, :, mine] = (stat[2:3, mine] * w_a + stat_rem[2:3, other] * w_b) * inv
        fac[NG + 2, :, mine] = w_a * inv
        fac[NG + 3, :, mine] = jnp.exp2((m_at[NG + 1, :, mine] - m_f) * C2) * inv

    def g_start(r, value):
        g_buf[r, my_slot[r]] = value
        for k in range(1, 8):
            send(
                g_buf.at[r, my_slot[r]], g_buf.at[r, my_slot[r]], g_s.at[r, k], g_r.at[r, my_slot[r]],
                partner(r, lax.rem(my_slot[r] + k, 8)),
            ).start()

    def g_wait(r):
        for k in range(1, 8):
            j = lax.rem(my_slot[r] + k, 8)
            send(
                g_buf.at[r, j], g_buf.at[r, j], g_s.at[r, k], g_r.at[r, j], partner(r, j)
            ).wait_recv()
        total = g_buf[r, 0]
        for k in range(1, 8):
            total = total + g_buf[r, k]
        return total

    def copy_ry(g, h):
        at_rows = pl.ds(h * HALF, HALF)
        return [
            send(
                y_out.at[g, sign, at_rows], y_in.at[g, sign, at_rows],
                ry_s.at[g, sign, h], ry_r.at[g, sign, h], ynb,
            )
            for sign in range(2)
        ]

    def copy_ry4(h):
        at_rows = pl.ds(h * HALF, HALF)
        return send(
            y_out.at[1, 0, at_rows], y_in.at[1, 0, at_rows], ry_s.at[1, 0, h], ry_r.at[1, 0, h], ynb
        )

    copy_ry0 = send(y_out.at[0, 0], y_in.at[0, 0], ry_s.at[0, 0, 0], ry_r.at[0, 0, 0], ynb)

    rz_plan = [
        (to, slot, h)
        for slot, to in ((0, 1), (1, -1), (2, 2), (3, -2), (4, 1), (5, -1))
        for h in (0, HALF)
    ] + [(2, 6, 0), (-2, 6, HALF)]
    rz_plan += [(to, slot, h) for slot, to in ((7, 1), (8, -1)) for h in (0, HALF)]

    def copy_rz(i):
        to, slot, h = rz_plan[i]
        at_slot = (slot, pl.ds(h, HALF))
        return send(z_out.at[at_slot], z_in.at[at_slot], rz_s.at[i], rz_r.at[i], z_dev(to))

    def gradients(g, at_rows):
        low = g + (NG + 3) * (1 - jnp.minimum(g, 1))
        dk = jnp.zeros((GR, DH), F32)
        dv = jnp.zeros((GR, DH), F32)
        for b in range(tiles):
            sl = tile(b)
            e = e_buf[at_rows, sl].astype(F32)
            p = jnp.concatenate([e[: GR // 2] * fac[g, :, sl], e[GR // 2 :] * fac[low, :, sl]], axis=0)
            pb = p.astype(BF)
            ds = (p * (dp_buf[at_rows, sl] - fac[NG + 1, :, sl])).astype(BF)
            dv = dv + dot(pb, do[sl, :], NN)
            dk = dk + dot(ds, q[sl, :], NN)
        part[g, :, 0:DH] = dk
        part[g, :, DH:] = dv

    gradients(NG - 1, last)
    y_out[3, 0] = part[3, 0:OWN, :].astype(BF)
    y_out[3, 1] = part[3, OWN : 2 * OWN, :].astype(BF)
    y_out[1, 0] = part[3, 3 * OWN :, :].astype(BF)
    for h in range(2):
        for c in copy_ry(3, h):
            c.start()
        copy_ry4(h).start()

    own = fac[NG + 2]
    ok_t[0:DH, :] = ok_t[0:DH, :] * own
    dq_t[...] = (dq_t[...] - ok_t[DH:, :] * fac[NG + 1]) * own
    copy_dq = send(dq_t.at[:, NQ:], dq_rem, c_s.at[4], c_r.at[4], sib)
    copy_dq.start()
    copy_o = send(ok_t.at[0:DH, NQ:], o_rem, c_s.at[3], c_r.at[3], sib)
    copy_o.start()
    pairs = dot(dq_t[...].astype(BF), q[...], NN)
    eye = lax.broadcasted_iota(jnp.int32, (DH, DH), 0) == lax.broadcasted_iota(jnp.int32, (DH, DH), 1)
    g_start(0, jnp.sum(jnp.where(eye, pairs, 0.0).reshape(DH // 8, 8, DH), axis=0))

    def far_sums(h):
        for c in copy_ry(3, h):
            c.wait_recv()
        copy_ry4(h).wait_recv()
        r = slice(h * HALF, (h + 1) * HALF)
        for sign in range(2):
            start = (2 + sign) * OWN + h * HALF
            z_out[4 + sign, r, :] = (
                part[2, start : start + HALF, :] + y_in[3, sign, r, :].astype(F32)
            ).astype(BF)
            copy_rz(8 + 2 * sign + h).start()
        start = 2 * OWN + h * HALF
        z_out[6, r, :] = (part[3, start : start + HALF, :] + y_in[1, 0, r, :].astype(F32)).astype(BF)
        copy_rz(12 + h).start()

    def backward(i, carry):
        g = NG - 2 - i
        gradients(g, pl.ds(pl.multiple_of(g * GR, GR), GR))

        @pl.when(g == 2)
        def _():
            z_out[7] = part[2, 0:OWN, :].astype(BF)
            z_out[8] = part[2, OWN : 2 * OWN, :].astype(BF)
            for j in range(14, 18):
                copy_rz(j).start()

        @pl.when(g == 1)
        def _():
            y_out[2, 0] = part[1, 0:OWN, :].astype(BF)
            y_out[2, 1] = part[1, OWN : 2 * OWN, :].astype(BF)
            for h in range(2):
                for c in copy_ry(2, h):
                    c.start()
            far_sums(0)

        return carry

    lax.fori_loop(0, NG - 1, backward, 0)

    far_sums(1)
    z_out[0] = part[0, 2 * OWN : 3 * OWN, :].astype(BF)
    z_out[1] = part[0, 3 * OWN :, :].astype(BF)
    for j in range(4):
        copy_rz(j).start()
    g_start(1, g_wait(0))

    dk = jnp.zeros((TOK, DH), F32)
    dv = jnp.zeros((TOK, DH), F32)
    for b in range(NQ // QB):
        sl = slice(b * QB, (b + 1) * QB)
        p = e_own[:, sl].astype(F32) * fac[NG, :, sl]
        pb = p.astype(BF)
        ds = (p * (dp_own[:, sl] - fac[NG + 1, :, sl])).astype(BF)
        dv = dv + dot(pb, do[sl, :], NN)
        dk = dk + dot(ds, q[sl, :], NN)
    dck[...] = norm_back(ck_raw, kg, dk * SCALE).astype(BF)
    dcv[...] = dv.astype(BF)
    writes = [
        pltpu.make_async_copy(dck, dck_hbm, io_s.at[2]),
        pltpu.make_async_copy(dcv, dcv_hbm, io_s.at[3]),
    ]
    for w in writes:
        w.start()

    copy_o.wait_recv()
    for h in range(QH):
        sl = slice(h * TOK, (h + 1) * TOK)
        x = (ok_t[0:DH, sl] + o_rem[:, sl]).T
        out[:, h * DH : (h + 1) * DH] = jnp.where(live_rows, x, 0.0).astype(BF)
    write_o = pltpu.make_async_copy(out, out_hbm, io_s.at[4])
    write_o.start()

    g_start(2, g_wait(1))
    for j in range(14, 18):
        copy_rz(j).wait_recv()
    y_out[0, 0] = (
        part[0, OWN : 2 * OWN, :] + z_in[7].astype(F32) + z_in[8].astype(F32)
    ).astype(BF)
    copy_ry0.start()
    for h in range(2):
        for c in copy_ry(2, h):
            c.wait_recv()
        copy_rz(8 + h).wait_recv()
        copy_rz(10 + h).wait_recv()
        copy_rz(12 + h).wait_recv()
        r = slice(h * HALF, (h + 1) * HALF)
        for sign in range(2):
            start = (2 + sign) * OWN + h * HALF
            acc = part[1, start : start + HALF, :] + y_in[2, sign, r, :].astype(F32)
            acc = acc + z_in[4 + sign, r, :].astype(F32)
            if sign == h:
                acc = acc + z_in[6, r, :].astype(F32)
            z_out[2 + sign, r, :] = acc.astype(BF)
            copy_rz(4 + 2 * sign + h).start()

    copy_dq.wait_recv()
    for h in range(QH):
        sl = slice(h * TOK, (h + 1) * TOK)
        up = (dq_t[:, sl] + dq_rem[:, sl]).T * SCALE
        x = cq[:, h * DH : (h + 1) * DH].astype(F32)
        dq[:, h * DH : (h + 1) * DH] = norm_back(x, qg, up).astype(BF)
    write_dq = pltpu.make_async_copy(dq, dq_hbm, io_s.at[5])
    write_dq.start()

    copy_ry0.wait_recv()
    for j in range(8):
        copy_rz(j).wait_recv()
    total = part[0, 0:OWN, :] + y_in[0, 0].astype(F32)
    for i in range(4):
        total = total + z_in[i].astype(F32)
    dpk[...] = norm_back(pk_raw, kg, total[:, 0:DH] * SCALE).astype(BF)
    dpv[...] = total[:, DH:].astype(BF)
    write_pk = pltpu.make_async_copy(dpk, dpk_hbm, io_s.at[6])
    write_pv = pltpu.make_async_copy(dpv, dpv_hbm, io_s.at[7])
    write_pk.start()
    write_pv.start()

    g_sum = jnp.sum(g_wait(2), axis=0, keepdims=True) * (SCALE / math.sqrt(GAIN_ROWS))
    gains[0:1, :] = g_sum / qg
    gains[1:2, :] = g_sum / kg
    write_g = pltpu.make_async_copy(gains, gains_hbm, io_s.at[8])
    write_g.start()

    for i in range(24):
        copy_z(i).wait_send()
    for i in range(18):
        copy_rz(i).wait_send()
    for i in range(6):
        copy_y(i).wait_send()
    for c in (copy_q, copy_do, copy_st, copy_o, copy_dq, copy_ry0):
        c.wait_send()
    for h in range(2):
        copy_ry4(h).wait_send()
        for c in copy_ry(2, h) + copy_ry(3, h):
            c.wait_send()
    for r in range(3):
        for k in range(1, 8):
            j = lax.rem(my_slot[r] + k, 8)
            send(
                g_buf.at[r, my_slot[r]], g_buf.at[r, my_slot[r]], g_s.at[r, k], g_r.at[r, j], partner(r, j)
            ).wait_send()
    for w in writes + [write_o, write_dq, write_pk, write_pv, write_g]:
        w.wait()


def place(*refs):
    count = (len(refs) - 1) // 3
    src, dst, held, sems = refs[:count], refs[count : 2 * count], refs[2 * count : 3 * count], refs[-1]
    reads = [pltpu.make_async_copy(src[i], held[i], sems.at[0, i]) for i in range(count)]
    writes = [pltpu.make_async_copy(held[i], dst[i], sems.at[1, i]) for i in range(count)]
    for r in reads:
        r.start()
    for r, w in zip(reads, writes):
        r.wait()
        w.start()
    for w in writes:
        w.wait()


GAIN_ROWS = 524288


def per_device(comp_q, comp_k, comp_v, prompt_k, prompt_v, lengths, q_gain, k_gain, d_out):
    dma = pltpu.SemaphoreType.DMA
    width = QH * DH
    shapes = [
        jax.ShapeDtypeStruct((TOK, width), BF),
        jax.ShapeDtypeStruct((TOK, width), BF),
        jax.ShapeDtypeStruct((TOK, DH), BF),
        jax.ShapeDtypeStruct((TOK, DH), BF),
        jax.ShapeDtypeStruct((OWN, DH), BF),
        jax.ShapeDtypeStruct((OWN, DH), BF),
        jax.ShapeDtypeStruct((2, DH), F32),
    ]
    scratch = [
        pltpu.VMEM((TOK, width), BF),
        pltpu.VMEM((TOK, DH), BF),
        pltpu.VMEM((TOK, DH), BF),
        pltpu.VMEM((OWN, DH), BF),
        pltpu.VMEM((OWN, DH), BF),
        pltpu.VMEM((1, 1), jnp.int32),
        pltpu.VMEM((1, DH), F32),
        pltpu.VMEM((1, DH), F32),
        pltpu.VMEM((TOK, width), BF),
        pltpu.VMEM((TOK, width), BF),
        pltpu.VMEM((TOK, width), BF),
        pltpu.VMEM((TOK, DH), BF),
        pltpu.VMEM((TOK, DH), BF),
        pltpu.VMEM((OWN, DH), BF),
        pltpu.VMEM((OWN, DH), BF),
        pltpu.VMEM((2, DH), F32),
        pltpu.VMEM((KEYS, 2 * DH), BF),
        pltpu.VMEM((Q2, DH), BF),
        pltpu.VMEM((Q2, DH), BF),
        pltpu.VMEM((TOK, 2 * DH), BF),
        pltpu.VMEM((2 * DH, GR), BF),
        pltpu.VMEM((2 * DH, GR // 2), BF),
        pltpu.VMEM((2 * DH, TOK), BF),
        pltpu.VMEM((GR, Q2), F32),
        pltpu.VMEM((KEYS, Q2), BF),
        pltpu.VMEM((GR, Q2), BF),
        pltpu.VMEM((KEYS, Q2), F32),
        pltpu.VMEM((TOK, NQ), BF),
        pltpu.VMEM((TOK, NQ), F32),
        pltpu.VMEM((2 * DH, Q2), F32),
        pltpu.VMEM((DH, Q2), F32),
        pltpu.VMEM((DH, NQ), F32),
        pltpu.VMEM((DH, NQ), F32),
        pltpu.VMEM((1, Q2), F32),
        pltpu.VMEM((NG + 2, 1, Q2), F32),
        pltpu.VMEM((8, Q2), F32),
        pltpu.VMEM((8, Q2), F32),
        pltpu.VMEM((NG + 4, 1, Q2), F32),
        pltpu.VMEM((NG, GR, 2 * DH), F32),
        pltpu.VMEM((NG, 2, OWN, 2 * DH), BF),
        pltpu.VMEM((NG, 2, OWN, 2 * DH), BF),
        pltpu.VMEM((9, OWN, 2 * DH), BF),
        pltpu.VMEM((9, OWN, 2 * DH), BF),
        pltpu.VMEM((3, 8, 8, DH), F32),
        dma((18,)), dma((24,)), dma((24,)), dma((6,)), dma((6,)), dma((5,)), dma((5,)),
        dma((NG, 2, 2)), dma((NG, 2, 2)), dma((18,)), dma((18,)), dma((3, 8)), dma((3, 8)),
    ]
    anywhere = pl.BlockSpec(memory_space=pl.ANY)
    res = pl.pallas_call(
        kernel,
        out_shape=shapes,
        in_specs=[anywhere] * 9,
        out_specs=[anywhere] * 7,
        scratch_shapes=scratch,
        compiler_params=pltpu.CompilerParams(
            collective_id=0, has_side_effects=True, vmem_limit_bytes=56 * 2**20
        ),
    )(
        comp_q.reshape(TOK, width),
        comp_k.reshape(TOK, DH),
        comp_v.reshape(TOK, DH),
        prompt_k.reshape(OWN, DH),
        prompt_v.reshape(OWN, DH),
        lengths,
        q_gain.reshape(1, DH),
        k_gain.reshape(1, DH),
        d_out.reshape(TOK, width),
    )
    res = pl.pallas_call(
        place,
        out_shape=shapes,
        in_specs=[anywhere] * 7,
        out_specs=[anywhere] * 7,
        scratch_shapes=[pltpu.VMEM(x.shape, x.dtype) for x in shapes] + [dma((2, 7))],
    )(*res)
    return (
        res[0].reshape(1, 1, TOK, width),
        res[1].reshape(1, 1, TOK, width),
        res[2].reshape(1, 1, TOK, DH),
        res[3].reshape(1, 1, TOK, DH),
        res[4].reshape(1, OWN, DH),
        res[5].reshape(1, OWN, DH),
        res[6],
    )


def solution(mesh):
    return jax.shard_map(
        per_device,
        mesh=mesh,
        in_specs=(
            P("prompt", "sample", None, "head"),
            P("prompt", "sample", None, "head"),
            P("prompt", "sample", None, "head"),
            P("prompt", "sample", "head"),
            P("prompt", "sample", "head"),
            P("prompt", "sample"),
            P(),
            P(),
            P("prompt", "sample", None, "head"),
        ),
        out_specs=(
            P("prompt", "sample", None, "head"),
            P("prompt", "sample", None, "head"),
            P("prompt", "sample", None, "head"),
            P("prompt", "sample", None, "head"),
            P("prompt", "sample", "head"),
            P("prompt", "sample", "head"),
            P(),
        ),
        check_vma=False,
    )
```

```python
import functools
import math

import jax
import jax.numpy as jnp
from jax import lax
from jax.experimental import pallas as pl
from jax.experimental.pallas import tpu as pltpu
from jax.sharding import PartitionSpec as P

EPS = 1e-06
BF = jnp.bfloat16
F32 = jnp.float32
NT = (((1,), (1,)), ((), ()))
NN = (((1,), (0,)), ((), ()))
DH = 128
TOK = 128
QH = 8
NQ = TOK * QH
Q2 = 2 * NQ
OWN = 96
GR = 4 * OWN
NG = 4
KEYS = NG * GR
QB = 256
SCALE = 1.0 / math.sqrt(DH)
C2 = SCALE / math.log(2.0)
LOW = -1e30
MESH = pl.DeviceIdType.MESH
FAR_FIRST = (4, 3, 5, 2, 6, 1, 7)


def dot(a, b, dims):
    return lax.dot_general(a, b, dims, preferred_element_type=F32)


def rms(x):
    return lax.rsqrt(jnp.mean(x * x, axis=-1, keepdims=True) + EPS)


def norm_back(x, gain, up):
    r = rms(x)
    g = up * gain
    return r * g - x * (r * r * r * jnp.mean(x * g, axis=-1, keepdims=True))


def row_near(d):
    return ((d - 1) * 4 + 2) * OWN


def row_far(d):
    return (8, 4, 12)[d - 1] * OWN


ROW_FAR0 = OWN
ROW_FAR4 = (3 * 4 + 3) * OWN
HALF = OWN // 2


def kernel(
    cq_hbm, ck_hbm, cv_hbm, pk_hbm, pv_hbm, live_hbm, q_gain_hbm, k_gain_hbm, dout_hbm,
    out_hbm, dq_hbm, dck_hbm, dcv_hbm, dpk_hbm, dpv_hbm, gains_hbm,
    cq, ck, cv, pk, pv, live_ref, q_gain, k_gain, d_out, out, dq, dck, dcv, dpk, dpv, gains,
    kv, q, do, ownkv, trans, trans_half, trans_own, s_buf, e_buf, f_buf, dp_buf, e_own, dp_own, ok_t, dq_t, o_rem, dq_rem, m_run,
    m_at, stat, stat_rem, fac, part, y_out, y_in, z_out, z_in, g_buf,
    io_s, za_s, za_r, y_s, y_r, c_s, c_r, ry_s, ry_r, rz_s, rz_r, g_s, g_r,
):
    reads = [
        pltpu.make_async_copy(src, dst, io_s.at[9 + i])
        for i, (src, dst) in enumerate(
            (
                (pk_hbm, pk), (k_gain_hbm, k_gain), (pv_hbm, pv), (cq_hbm, cq), (q_gain_hbm, q_gain),
                (live_hbm, live_ref), (dout_hbm, d_out), (ck_hbm, ck), (cv_hbm, cv),
            )
        )
    ]
    for r in reads:
        r.start()

    sample = lax.axis_index("sample")
    px = lax.axis_index("prompt")
    hy = lax.axis_index("head")
    core = lax.rem(sample, 2)
    y = lax.rem(sample // 2, 2)
    z = sample // 4

    def at(z_, y_, c_):
        return z_ * 4 + y_ * 2 + c_

    sib = {"sample": at(z, y, 1 - core)}
    ynb = {"sample": at(z, 1 - y, core)}

    def z_dev(d):
        return {"sample": at(lax.rem(z + d + 8, 8), y, core)}

    my_slot = (px * 2 + core, z, hy * 2 + y)

    def partner(r, i):
        if r == 0:
            return {"prompt": i // 2, "sample": at(z, y, lax.rem(i, 2))}
        if r == 1:
            return {"sample": at(i, y, core)}
        return {"head": i // 2, "sample": at(z, lax.rem(i, 2), core)}

    def send(src, dst, ss, rs, dev):
        return pltpu.make_async_remote_copy(
            src_ref=src, dst_ref=dst, send_sem=ss, recv_sem=rs, device_id=dev, device_id_type=MESH
        )

    barrier = pltpu.get_barrier_semaphore()
    for k in FAR_FIRST:
        for r in (1, 2, 0):
            pl.semaphore_signal(
                barrier, inc=1, device_id=partner(r, lax.rem(my_slot[r] + k, 8)), device_id_type=MESH
            )

    for r in reads[0:3]:
        r.wait()
    kg = k_gain[...]
    pk_raw = pk[...].astype(F32)
    kv[0:OWN, 0:DH] = (pk_raw * rms(pk_raw) * kg).astype(BF)
    kv[0:OWN, DH:] = pv[...]
    pl.semaphore_wait(barrier, 21)

    def rows(start, count=OWN):
        return kv.at[pl.ds(start, count), :]

    def halves(to, dst, src):
        return [(to, dst, src), (to, dst + HALF, src + HALF)]

    z_plan = (
        halves(-1, row_near(1), 0)
        + halves(1, row_near(1) + OWN, 0)
        + halves(-2, row_near(2), 0)
        + halves(2, row_near(2) + OWN, 0)
        + halves(-1, row_near(3), row_near(2))
        + halves(1, row_near(3) + OWN, row_near(2) + OWN)
        + [(-2, row_near(4), row_near(2)), (2, row_near(4) + HALF, row_near(2) + OWN + HALF)]
        + halves(-2, row_far(2), ROW_FAR0)
        + halves(2, row_far(2) + OWN, ROW_FAR0)
        + halves(-1, row_far(3), row_far(2))
        + halves(1, row_far(3) + OWN, row_far(2) + OWN)
        + [(-2, ROW_FAR4, row_far(2)), (2, ROW_FAR4 + HALF, row_far(2) + OWN + HALF)]
    )

    def copy_z(i):
        to, dst, src = z_plan[i]
        return send(rows(src, HALF), rows(dst, HALF), za_s.at[i], za_r.at[i], z_dev(to))

    y_plan = [
        (dst + h, src + h)
        for dst, src in (
            (ROW_FAR0, 0),
            (row_far(1), row_near(1)),
            (row_far(1) + OWN, row_near(1) + OWN),
        )
        for h in (0, HALF)
    ]

    def copy_y(i):
        dst, src = y_plan[i]
        return send(rows(src, HALF), rows(dst, HALF), y_s.at[i], y_r.at[i], ynb)

    copy_y(0).start()
    copy_y(1).start()
    for i in (4, 6, 5, 7, 0, 2, 1, 3):
        copy_z(i).start()

    for r in reads[3:6]:
        r.wait()
    qg = q_gain[...]
    live_rows = lax.broadcasted_iota(jnp.int32, (TOK, 1), 0) < live_ref[...]
    for h in range(QH):
        x = cq[:, h * DH : (h + 1) * DH].astype(F32)
        q[h * TOK : (h + 1) * TOK, :] = (x * rms(x) * qg).astype(BF)
    copy_q = send(q.at[0:NQ, :], q.at[NQ:, :], c_s.at[0], c_r.at[0], sib)
    copy_q.start()
    reads[6].wait()
    for h in range(QH):
        g = d_out[:, h * DH : (h + 1) * DH]
        do[h * TOK : (h + 1) * TOK, :] = jnp.where(live_rows, g, jnp.zeros_like(g))
    copy_do = send(do.at[0:NQ, :], do.at[NQ:, :], c_s.at[1], c_r.at[1], sib)
    copy_do.start()

    reads[7].wait()
    reads[8].wait()
    ck_raw = ck[...].astype(F32)
    ownkv[:, 0:DH] = (ck_raw * rms(ck_raw) * kg).astype(BF)
    ownkv[:, DH:] = cv[...]

    def turn(keys, vals, into):
        into[0:DH, :] = vals.astype(F32).T.astype(BF)
        into[DH:, :] = keys.astype(F32).T.astype(BF)

    m_run[...] = jnp.full((1, Q2), LOW, F32)
    stat[...] = jnp.zeros((8, Q2), F32)
    ok_t[:, NQ:] = jnp.zeros((2 * DH, NQ), F32)
    dq_t[:, NQ:] = jnp.zeros((DH, NQ), F32)
    turn(ownkv[:, 0:DH], ownkv[:, DH:], trans_own)
    u_ids = lax.broadcasted_iota(jnp.int32, (TOK, QB), 0)
    t_ids = lax.rem(lax.broadcasted_iota(jnp.int32, (TOK, QB), 1), TOK)
    allowed = u_ids <= t_ids
    for b in range(NQ // QB):
        sl = slice(b * QB, (b + 1) * QB)
        s = jnp.where(allowed, dot(ownkv[:, 0:DH], q[sl, :], NT), LOW)
        dp = dot(ownkv[:, DH:], do[sl, :], NT)
        m = jnp.max(s, axis=0, keepdims=True)
        e = jnp.exp2((s - m) * C2)
        eb = e.astype(BF)
        ed = e * dp
        e_own[:, sl] = eb
        dp_own[:, sl] = dp
        m_run[:, sl] = m
        stat[1:2, sl] = jnp.sum(e, axis=0, keepdims=True)
        stat[2:3, sl] = jnp.sum(ed, axis=0, keepdims=True)
        ok_t[:, sl] = dot(trans_own[...], eb, NN)
        dq_t[:, sl] = dot(trans_own[DH:, :], ed.astype(BF), NN)
    m_at[NG] = m_run[...]

    for h in range(2):
        copy_y(h).wait_recv()
        copy_z(14 + h).start()
        copy_z(16 + h).start()
    copy_q.wait_recv()
    copy_do.wait_recv()

    tiles = Q2 // QB

    def tile(b):
        return slice(b * QB, (b + 1) * QB)

    def rise(b, mx):
        m_old = m_run[:, tile(b)]
        m_new = jnp.maximum(m_old, mx)
        m_run[:, tile(b)] = m_new
        return jnp.exp2((m_old - m_new) * C2), m_new * C2

    def scores(b, at_rows, keys, vals):
        s = dot(keys, q[tile(b), :], NT)
        s_buf[0 : keys.shape[0], tile(b)] = s
        dp_buf[at_rows, tile(b)] = dot(vals, do[tile(b), :], NT)
        return jnp.max(s, axis=0, keepdims=True)

    def weigh(b, at_rows, al, mc, count):
        sl = tile(b)
        e = jnp.exp2(s_buf[0:count, sl] * C2 - mc)
        ed = e * dp_buf[at_rows, sl]
        e_buf[at_rows, sl] = e.astype(BF)
        f_buf[0:count, sl] = ed.astype(BF)
        stat[1:2, sl] = stat[1:2, sl] * al + jnp.sum(e, axis=0, keepdims=True)
        stat[2:3, sl] = stat[2:3, sl] * al + jnp.sum(ed, axis=0, keepdims=True)

    def mix(b, at_rows, al, turned, count):
        sl = tile(b)
        ok_t[:, sl] = ok_t[:, sl] * al + dot(turned[...], e_buf[at_rows, sl], NN)
        dq_t[:, sl] = dq_t[:, sl] * al + dot(turned[DH:, :], f_buf[0:count, sl], NN)

    def attend(at_rows, turned, count):
        keys = kv[at_rows, 0:DH]
        vals = kv[at_rows, DH:]
        turn(keys, vals, turned)
        mx, al, mc = {}, {}, {}
        for t in range(tiles + 2):
            if 1 <= t <= tiles:
                al[t - 1], mc[t - 1] = rise(t - 1, mx[t - 1])
            if t < tiles:
                mx[t] = scores(t, at_rows, keys, vals)
            if 1 <= t <= tiles:
                weigh(t - 1, at_rows, al[t - 1], mc[t - 1], count)
            if t >= 2:
                mix(t - 2, at_rows, al[t - 2], turned, count)

    def forward_half(i, carry):
        @pl.when(i == 1)
        def _():
            for h in range(2):
                copy_z(4 + h).wait_recv()
                copy_z(6 + h).wait_recv()
                for i in (8 + h, 12 + h, 10 + h):
                    copy_z(i).start()
            for h in range(2):
                copy_z(h).wait_recv()
                copy_z(2 + h).wait_recv()
                copy_y(2 + h).start()
                copy_y(4 + h).start()

        attend(pl.ds(pl.multiple_of(i * (GR // 2), GR // 2), GR // 2), trans_half, GR // 2)
        m_at[i * (NG + 1)] = m_run[...]
        return carry

    lax.fori_loop(0, 2, forward_half, 0)

    def forward(g, carry):
        @pl.when(g == 1)
        def _():
            for h in range(2):
                copy_z(14 + h).wait_recv()
                copy_z(16 + h).wait_recv()
                for j in (18 + h, 20 + h, 22 + h):
                    copy_z(j).start()

        @pl.when(g == 2)
        def _():
            for i in range(2, 6):
                copy_y(i).wait_recv()
            for i in range(8, 12):
                copy_z(i).wait_recv()

        attend(pl.ds(pl.multiple_of(g * GR, GR), GR), trans, GR)
        m_at[g] = m_run[...]
        return carry

    lax.fori_loop(1, NG - 1, forward, 0)

    for i in (12, 13, 18, 19, 20, 21, 22, 23):
        copy_z(i).wait_recv()
    last = slice((NG - 1) * GR, NG * GR)
    keys = kv[last, 0:DH]
    vals = kv[last, DH:]
    mx, al, mc = {}, {}, {}
    for t in range(tiles + 1):
        if t >= 1:
            al[t - 1], mc[t - 1] = rise(t - 1, mx[t - 1])
        if t < tiles:
            mx[t] = scores(t, last, keys, vals)
        if t >= 1:
            weigh(t - 1, last, al[t - 1], mc[t - 1], GR)
    m_at[NG - 1] = m_run[...]

    stat[0:1, :] = m_run[...]
    copy_st = send(stat, stat_rem, c_s.at[2], c_r.at[2], sib)
    copy_st.start()
    turn(keys, vals, trans)
    for b in range(tiles):
        mix(b, last, al[b], trans, GR)
    copy_st.wait_recv()
    for half in range(2):
        mine = slice(half * NQ, (half + 1) * NQ)
        other = slice((1 - half) * NQ, (2 - half) * NQ)
        m_a, m_b = stat[0:1, mine], stat_rem[0:1, other]
        m_f = jnp.maximum(m_a, m_b)
        w_a, w_b = jnp.exp2((m_a - m_f) * C2), jnp.exp2((m_b - m_f) * C2)
        inv = 1.0 / (stat[1:2, mine] * w_a + stat_rem[1:2, other] * w_b)
        for i in range(NG + (1 - half)):
            fac[i, :, mine] = jnp.exp2((m_at[i, :, mine] - m_f) * C2) * inv
        fac[NG + 1, :, mine] = (stat[2:3, mine] * w_a + stat_rem[2:3, other] * w_b) * inv
        fac[NG + 2, :, mine] = w_a * inv
        fac[NG + 3, :, mine] = jnp.exp2((m_at[NG + 1, :, mine] - m_f) * C2) * inv

    def g_start(r, value):
        g_buf[r, my_slot[r]] = value
        for k in FAR_FIRST:
            send(
                g_buf.at[r, my_slot[r]], g_buf.at[r, my_slot[r]], g_s.at[r, k], g_r.at[r, my_slot[r]],
                partner(r, lax.rem(my_slot[r] + k, 8)),
            ).start()

    def g_wait(r):
        for k in range(1, 8):
            j = lax.rem(my_slot[r] + k, 8)
            send(
                g_buf.at[r, j], g_buf.at[r, j], g_s.at[r, k], g_r.at[r, j], partner(r, j)
            ).wait_recv()
        total = g_buf[r, 0]
        for k in range(1, 8):
            total = total + g_buf[r, k]
        return total

    def copy_ry(g, h):
        at_rows = pl.ds(h * HALF, HALF)
        return [
            send(
                y_out.at[g, sign, at_rows], y_in.at[g, sign, at_rows],
                ry_s.at[g, sign, h], ry_r.at[g, sign, h], ynb,
            )
            for sign in range(2)
        ]

    def copy_ry4(h):
        at_rows = pl.ds(h * HALF, HALF)
        return send(
            y_out.at[1, 0, at_rows], y_in.at[1, 0, at_rows], ry_s.at[1, 0, h], ry_r.at[1, 0, h], ynb
        )

    copy_ry0 = send(y_out.at[0, 0], y_in.at[0, 0], ry_s.at[0, 0, 0], ry_r.at[0, 0, 0], ynb)

    rz_plan = [
        (to, slot, h)
        for slot, to in ((0, 1), (1, -1), (2, 2), (3, -2), (4, 1), (5, -1))
        for h in (0, HALF)
    ] + [(2, 6, 0), (-2, 6, HALF)]
    rz_plan += [(to, slot, h) for slot, to in ((7, 1), (8, -1)) for h in (0, HALF)]

    def copy_rz(i):
        to, slot, h = rz_plan[i]
        at_slot = (slot, pl.ds(h, HALF))
        return send(z_out.at[at_slot], z_in.at[at_slot], rz_s.at[i], rz_r.at[i], z_dev(to))

    def gradients(g, at_rows):
        low = g + (NG + 3) * (1 - jnp.minimum(g, 1))
        dk = jnp.zeros((GR, DH), F32)
        dv = jnp.zeros((GR, DH), F32)
        for b in range(tiles):
            sl = tile(b)
            e = e_buf[at_rows, sl].astype(F32)
            p = jnp.concatenate([e[: GR // 2] * fac[g, :, sl], e[GR // 2 :] * fac[low, :, sl]], axis=0)
            pb = p.astype(BF)
            ds = (p * (dp_buf[at_rows, sl] - fac[NG + 1, :, sl])).astype(BF)
            dv = dv + dot(pb, do[sl, :], NN)
            dk = dk + dot(ds, q[sl, :], NN)
        part[g, :, 0:DH] = dk
        part[g, :, DH:] = dv

    gradients(NG - 1, last)
    y_out[3, 0] = part[3, 0:OWN, :].astype(BF)
    y_out[3, 1] = part[3, OWN : 2 * OWN, :].astype(BF)
    y_out[1, 0] = part[3, 3 * OWN :, :].astype(BF)
    for h in range(2):
        copy_ry4(h).start()
        for c in copy_ry(3, h):
            c.start()

    own = fac[NG + 2]
    ok_t[0:DH, :] = ok_t[0:DH, :] * own
    dq_t[...] = (dq_t[...] - ok_t[DH:, :] * fac[NG + 1]) * own
    copy_dq = send(dq_t.at[:, NQ:], dq_rem, c_s.at[4], c_r.at[4], sib)
    copy_dq.start()
    copy_o = send(ok_t.at[0:DH, NQ:], o_rem, c_s.at[3], c_r.at[3], sib)
    copy_o.start()
    pairs = dot(dq_t[...].astype(BF), q[...], NN)
    eye = lax.broadcasted_iota(jnp.int32, (DH, DH), 0) == lax.broadcasted_iota(jnp.int32, (DH, DH), 1)
    g_start(0, jnp.sum(jnp.where(eye, pairs, 0.0).reshape(DH // 8, 8, DH), axis=0))

    def far_sums(h):
        r = slice(h * HALF, (h + 1) * HALF)
        copy_ry4(h).wait_recv()
        start = 2 * OWN + h * HALF
        z_out[6, r, :] = (part[3, start : start + HALF, :] + y_in[1, 0, r, :].astype(F32)).astype(BF)
        copy_rz(12 + h).start()
        for sign, c in enumerate(copy_ry(3, h)):
            c.wait_recv()
            start = (2 + sign) * OWN + h * HALF
            z_out[4 + sign, r, :] = (
                part[2, start : start + HALF, :] + y_in[3, sign, r, :].astype(F32)
            ).astype(BF)
            copy_rz(8 + 2 * sign + h).start()

    def backward(i, carry):
        g = NG - 2 - i
        gradients(g, pl.ds(pl.multiple_of(g * GR, GR), GR))

        @pl.when(g == 2)
        def _():
            z_out[7] = part[2, 0:OWN, :].astype(BF)
            z_out[8] = part[2, OWN : 2 * OWN, :].astype(BF)
            for j in range(14, 18):
                copy_rz(j).start()

        @pl.when(g == 1)
        def _():
            y_out[2, 0] = part[1, 0:OWN, :].astype(BF)
            y_out[2, 1] = part[1, OWN : 2 * OWN, :].astype(BF)
            for h in range(2):
                for c in copy_ry(2, h):
                    c.start()
            far_sums(0)

        return carry

    lax.fori_loop(0, NG - 1, backward, 0)

    g_start(1, g_wait(0))
    far_sums(1)
    z_out[0] = part[0, 2 * OWN : 3 * OWN, :].astype(BF)
    z_out[1] = part[0, 3 * OWN :, :].astype(BF)
    for j in range(4):
        copy_rz(j).start()

    dk = jnp.zeros((TOK, DH), F32)
    dv = jnp.zeros((TOK, DH), F32)
    for b in range(NQ // QB):
        sl = slice(b * QB, (b + 1) * QB)
        p = e_own[:, sl].astype(F32) * fac[NG, :, sl]
        pb = p.astype(BF)
        ds = (p * (dp_own[:, sl] - fac[NG + 1, :, sl])).astype(BF)
        dv = dv + dot(pb, do[sl, :], NN)
        dk = dk + dot(ds, q[sl, :], NN)
    dck[...] = norm_back(ck_raw, kg, dk * SCALE).astype(BF)
    dcv[...] = dv.astype(BF)
    writes = [
        pltpu.make_async_copy(dck, dck_hbm, io_s.at[2]),
        pltpu.make_async_copy(dcv, dcv_hbm, io_s.at[3]),
    ]
    for w in writes:
        w.start()

    copy_o.wait_recv()
    for h in range(QH):
        sl = slice(h * TOK, (h + 1) * TOK)
        x = (ok_t[0:DH, sl] + o_rem[:, sl]).T
        out[:, h * DH : (h + 1) * DH] = jnp.where(live_rows, x, 0.0).astype(BF)
    write_o = pltpu.make_async_copy(out, out_hbm, io_s.at[4])
    write_o.start()

    for j in range(14, 18):
        copy_rz(j).wait_recv()
    y_out[0, 0] = (
        part[0, OWN : 2 * OWN, :] + z_in[7].astype(F32) + z_in[8].astype(F32)
    ).astype(BF)
    copy_ry0.start()
    for h in range(2):
        for c in copy_ry(2, h):
            c.wait_recv()
        copy_rz(8 + h).wait_recv()
        copy_rz(10 + h).wait_recv()
        copy_rz(12 + h).wait_recv()
        r = slice(h * HALF, (h + 1) * HALF)
        for sign in range(2):
            start = (2 + sign) * OWN + h * HALF
            acc = part[1, start : start + HALF, :] + y_in[2, sign, r, :].astype(F32)
            acc = acc + z_in[4 + sign, r, :].astype(F32)
            if sign == h:
                acc = acc + z_in[6, r, :].astype(F32)
            z_out[2 + sign, r, :] = acc.astype(BF)
            copy_rz(4 + 2 * sign + h).start()

    g_start(2, g_wait(1))
    copy_dq.wait_recv()
    for h in range(QH):
        sl = slice(h * TOK, (h + 1) * TOK)
        up = (dq_t[:, sl] + dq_rem[:, sl]).T * SCALE
        x = cq[:, h * DH : (h + 1) * DH].astype(F32)
        dq[:, h * DH : (h + 1) * DH] = norm_back(x, qg, up).astype(BF)
    write_dq = pltpu.make_async_copy(dq, dq_hbm, io_s.at[5])
    write_dq.start()

    copy_ry0.wait_recv()
    for j in range(8):
        copy_rz(j).wait_recv()
    total = part[0, 0:OWN, :] + y_in[0, 0].astype(F32)
    for i in range(4):
        total = total + z_in[i].astype(F32)
    dpk[...] = norm_back(pk_raw, kg, total[:, 0:DH] * SCALE).astype(BF)
    dpv[...] = total[:, DH:].astype(BF)
    write_pk = pltpu.make_async_copy(dpk, dpk_hbm, io_s.at[6])
    write_pv = pltpu.make_async_copy(dpv, dpv_hbm, io_s.at[7])
    write_pk.start()
    write_pv.start()

    g_sum = jnp.sum(g_wait(2), axis=0, keepdims=True) * (SCALE / math.sqrt(GAIN_ROWS))
    gains[0:1, :] = g_sum / qg
    gains[1:2, :] = g_sum / kg
    write_g = pltpu.make_async_copy(gains, gains_hbm, io_s.at[8])
    write_g.start()

    for i in range(24):
        copy_z(i).wait_send()
    for i in range(18):
        copy_rz(i).wait_send()
    for i in range(6):
        copy_y(i).wait_send()
    for c in (copy_q, copy_do, copy_st, copy_o, copy_dq, copy_ry0):
        c.wait_send()
    for h in range(2):
        copy_ry4(h).wait_send()
        for c in copy_ry(2, h) + copy_ry(3, h):
            c.wait_send()
    for r in range(3):
        for k in range(1, 8):
            j = lax.rem(my_slot[r] + k, 8)
            send(
                g_buf.at[r, my_slot[r]], g_buf.at[r, my_slot[r]], g_s.at[r, k], g_r.at[r, j], partner(r, j)
            ).wait_send()
    for w in writes + [write_o, write_dq, write_pk, write_pv, write_g]:
        w.wait()


def place(*refs):
    count = (len(refs) - 1) // 3
    src, dst, held, sems = refs[:count], refs[count : 2 * count], refs[2 * count : 3 * count], refs[-1]
    reads = [pltpu.make_async_copy(src[i], held[i], sems.at[0, i]) for i in range(count)]
    writes = [pltpu.make_async_copy(held[i], dst[i], sems.at[1, i]) for i in range(count)]
    for r in reads:
        r.start()
    for r, w in zip(reads, writes):
        r.wait()
        w.start()
    for w in writes:
        w.wait()


GAIN_ROWS = 524288


def per_device(comp_q, comp_k, comp_v, prompt_k, prompt_v, lengths, q_gain, k_gain, d_out):
    dma = pltpu.SemaphoreType.DMA
    width = QH * DH
    shapes = [
        jax.ShapeDtypeStruct((TOK, width), BF),
        jax.ShapeDtypeStruct((TOK, width), BF),
        jax.ShapeDtypeStruct((TOK, DH), BF),
        jax.ShapeDtypeStruct((TOK, DH), BF),
        jax.ShapeDtypeStruct((OWN, DH), BF),
        jax.ShapeDtypeStruct((OWN, DH), BF),
        jax.ShapeDtypeStruct((2, DH), F32),
    ]
    scratch = [
        pltpu.VMEM((TOK, width), BF),
        pltpu.VMEM((TOK, DH), BF),
        pltpu.VMEM((TOK, DH), BF),
        pltpu.VMEM((OWN, DH), BF),
        pltpu.VMEM((OWN, DH), BF),
        pltpu.VMEM((1, 1), jnp.int32),
        pltpu.VMEM((1, DH), F32),
        pltpu.VMEM((1, DH), F32),
        pltpu.VMEM((TOK, width), BF),
        pltpu.VMEM((TOK, width), BF),
        pltpu.VMEM((TOK, width), BF),
        pltpu.VMEM((TOK, DH), BF),
        pltpu.VMEM((TOK, DH), BF),
        pltpu.VMEM((OWN, DH), BF),
        pltpu.VMEM((OWN, DH), BF),
        pltpu.VMEM((2, DH), F32),
        pltpu.VMEM((KEYS, 2 * DH), BF),
        pltpu.VMEM((Q2, DH), BF),
        pltpu.VMEM((Q2, DH), BF),
        pltpu.VMEM((TOK, 2 * DH), BF),
        pltpu.VMEM((2 * DH, GR), BF),
        pltpu.VMEM((2 * DH, GR // 2), BF),
        pltpu.VMEM((2 * DH, TOK), BF),
        pltpu.VMEM((GR, Q2), F32),
        pltpu.VMEM((KEYS, Q2), BF),
        pltpu.VMEM((GR, Q2), BF),
        pltpu.VMEM((KEYS, Q2), F32),
        pltpu.VMEM((TOK, NQ), BF),
        pltpu.VMEM((TOK, NQ), F32),
        pltpu.VMEM((2 * DH, Q2), F32),
        pltpu.VMEM((DH, Q2), F32),
        pltpu.VMEM((DH, NQ), F32),
        pltpu.VMEM((DH, NQ), F32),
        pltpu.VMEM((1, Q2), F32),
        pltpu.VMEM((NG + 2, 1, Q2), F32),
        pltpu.VMEM((8, Q2), F32),
        pltpu.VMEM((8, Q2), F32),
        pltpu.VMEM((NG + 4, 1, Q2), F32),
        pltpu.VMEM((NG, GR, 2 * DH), F32),
        pltpu.VMEM((NG, 2, OWN, 2 * DH), BF),
        pltpu.VMEM((NG, 2, OWN, 2 * DH), BF),
        pltpu.VMEM((9, OWN, 2 * DH), BF),
        pltpu.VMEM((9, OWN, 2 * DH), BF),
        pltpu.VMEM((3, 8, 8, DH), F32),
        dma((18,)), dma((24,)), dma((24,)), dma((6,)), dma((6,)), dma((5,)), dma((5,)),
        dma((NG, 2, 2)), dma((NG, 2, 2)), dma((18,)), dma((18,)), dma((3, 8)), dma((3, 8)),
    ]
    anywhere = pl.BlockSpec(memory_space=pl.ANY)
    res = pl.pallas_call(
        kernel,
        out_shape=shapes,
        in_specs=[anywhere] * 9,
        out_specs=[anywhere] * 7,
        scratch_shapes=scratch,
        compiler_params=pltpu.CompilerParams(
            collective_id=0, has_side_effects=True, vmem_limit_bytes=56 * 2**20
        ),
    )(
        comp_q.reshape(TOK, width),
        comp_k.reshape(TOK, DH),
        comp_v.reshape(TOK, DH),
        prompt_k.reshape(OWN, DH),
        prompt_v.reshape(OWN, DH),
        lengths,
        q_gain.reshape(1, DH),
        k_gain.reshape(1, DH),
        d_out.reshape(TOK, width),
    )
    res = pl.pallas_call(
        place,
        out_shape=shapes,
        in_specs=[anywhere] * 7,
        out_specs=[anywhere] * 7,
        scratch_shapes=[pltpu.VMEM(x.shape, x.dtype) for x in shapes] + [dma((2, 7))],
    )(*res)
    return (
        res[0].reshape(1, 1, TOK, width),
        res[1].reshape(1, 1, TOK, width),
        res[2].reshape(1, 1, TOK, DH),
        res[3].reshape(1, 1, TOK, DH),
        res[4].reshape(1, OWN, DH),
        res[5].reshape(1, OWN, DH),
        res[6],
    )


def solution(mesh):
    return jax.shard_map(
        per_device,
        mesh=mesh,
        in_specs=(
            P("prompt", "sample", None, "head"),
            P("prompt", "sample", None, "head"),
            P("prompt", "sample", None, "head"),
            P("prompt", "sample", "head"),
            P("prompt", "sample", "head"),
            P("prompt", "sample"),
            P(),
            P(),
            P("prompt", "sample", None, "head"),
        ),
        out_specs=(
            P("prompt", "sample", None, "head"),
            P("prompt", "sample", None, "head"),
            P("prompt", "sample", None, "head"),
            P("prompt", "sample", None, "head"),
            P("prompt", "sample", "head"),
            P("prompt", "sample", "head"),
            P(),
        ),
        check_vma=False,
    )
```
